512 devices in a mesh: row: 16 (over x_lo, y), col: 32 (over x_hi, z, core).
Axes of the slice: x: 4 (x_hi: 2, x_lo: 2; x = x_hi * 2 + x_lo), y: 8, z: 8, core: 2. Of those that a mesh axis runs over, the one named last changes fastest.
Arguments:
- weight: bfloat16 [8192, 28672], P('row', 'col'), may hold values from -6 to 6
- eigenbasis: bfloat16 [28672, 28672], P('col', 'row'), may hold values from -0.03125 to 0.03125
- eigenvalues: float32 [28672], P('row'), may hold values from 0 to 10, as said below
- removed_local: int32 [32, 36], P('col'), may hold values from 0 to 895, as said below
- counts: int32 [32], replicated, may hold values from 1 to 36, 768 in all
Outputs:
- pruned: bfloat16 [8192, 28672], P('row', 'col')
The draws below stay inside these ranges and needn't reach their ends.
Inputs may be any that keep to these rules, and one draw needn't show every extreme that they name: `removed_local`: row s holds distinct unit numbers of column shard s; its first counts[s] entries are that shard's removed units. The counts sum to 768; some shard removes exactly 36 units. `eigenvalues`: every entry is positive.
All inputs are finite; a program needn't handle non-finite values.
Results may differ from the reference program's by a relative error of at most 0.0075.
The reference program's roundings to bfloat16 on the way (of `scaled`, `solved_half` and `rows_half`) count: a program that leaves them out, or rounds other values in their place, can miss the bound.
Values may be sent and summed in bfloat16 or wider, within the bound.
A program may use at most 64 MiB of HBM per device.

```python
import math
import jax
import jax.numpy as jnp
import numpy as np
from jax import lax

D = 8192
FF = 28672
KMAX = 36
K = 768
N_COL = 32


def draw_removed_local(key, part):
    shard_width = FF // N_COL
    row_keys = jax.random.split(key, N_COL)
    shuffles = jax.vmap(lambda row_key: jax.random.permutation(row_key, shard_width))(row_keys)
    marked = jax.random.randint(jax.random.fold_in(key, 7), (), 0, N_COL)
    row_ids = jnp.arange(N_COL)
    leaders = shuffles[:, 0]
    offsets = jnp.where(row_ids == marked, shard_width - 1 - leaders, jnp.where(row_ids == (marked + 1) % N_COL, shard_width - leaders, 0))
    return ((shuffles + offsets[:, None]) % shard_width)[:, :KMAX].astype(jnp.int32)


def draw_eigenvalues(key, part):
    heavy = jax.random.permutation(jax.random.fold_in(key, 3), FF) < K
    spread_key = jax.random.fold_in(key, 5)
    factor_key = jax.random.fold_in(key, 9)
    bulk = jnp.exp(jax.random.uniform(spread_key, (FF,), jnp.float32, math.log(0.1), math.log(10.0)))
    level = 2.1498
    factor = jnp.exp(jax.random.uniform(factor_key, (FF,), jnp.float32, math.log(0.75), math.log(3.0)))
    small = K / (16.0 * level * FF) / factor
    return jnp.where(heavy, small, bulk).astype(jnp.float32)


def level_of(own_key, shape, pieces, least, high):
    level = 1.0
    for position, blocks in pieces:
        steps = jax.random.uniform(jax.random.fold_in(jax.random.fold_in(own_key, 6), position), (blocks,), jnp.float32, least / len(pieces), high / len(pieces))
        level = level * jnp.repeat(jnp.exp(steps), shape[position] // blocks).reshape((-1,) + (1,) * (len(shape) - 1 - position))
    return level


def profile(amount, total, bound, skew):
    portions = [(1 << 20) // math.isqrt(standing ** skew) + 1 for standing in range(2, amount + 1)]
    surplus, given = total - bound - (amount - 1), [1] * (amount - 1)
    while surplus > 0:
        free = [i for i in range(amount - 1) if given[i] < bound]
        pool, left = sum([portions[i] for i in free]), surplus
        for i in free:
            extra = min(bound - given[i], max(1, left * portions[i] // pool), surplus)
            given[i] = given[i] + extra
            surplus = surplus - extra
    return np.array([bound] + given)


def ragged_sizes(rng, number_of, total, reach, slope):
    if number_of == 2:
        one = jax.random.randint(rng, (), max(1, total - reach), min(reach, total - 1) + 1)
        return jnp.stack([one, total - one])
    sizes = jnp.asarray(profile(number_of, total, reach, slope), jnp.int32)
    couples = (number_of - 1) // 2
    source_of, sink = sizes[1:1 + 2 * couples:2], sizes[2:2 + 2 * couples:2]
    slack = jnp.minimum(source_of - 1, reach - sink)
    shifted = jax.random.randint(jax.random.fold_in(rng, 1), (couples,), 0, 1 << 20) % (slack + 1)
    sizes = sizes.at[1:1 + 2 * couples:2].set(source_of - shifted).at[2:2 + 2 * couples:2].set(sink + shifted)
    return sizes[jax.random.permutation(jax.random.fold_in(rng, 2), number_of)]


def bell_draw(rng, extent, deviation, limit, cuts=(), kind=jnp.bfloat16):
    entries = deviation * jax.random.normal(rng, extent, jnp.float32)
    if cuts:
        entries = entries * level_of(rng, extent, cuts, -0.22, 0.18)
    return jnp.clip(entries, -limit, limit).astype(kind)


def setup_inputs(seed: int = 0) -> dict:
    key_list = jax.random.split(jax.random.key(seed), 6)
    return {
        "weight": bell_draw(key_list[0], (D, FF), 1.0, 6.0, ((0, 16), (1, 32))),
        "eigenbasis": bell_draw(key_list[1], (FF, FF), FF ** -0.5, 0.03125, ((0, 32), (1, 16))),
        "eigenvalues": draw_eigenvalues(jax.random.fold_in(key_list[5], 71), 0),
        "removed_local": draw_removed_local(jax.random.fold_in(key_list[5], 71), 0),
        "counts": ragged_sizes(key_list[4], N_COL, K, KMAX, 2).astype(jnp.int32),
    }


def compact_index(counts, removed_count, slot_count):
    shard_ends = jnp.cumsum(counts).astype(jnp.int32)
    shard_starts = shard_ends - counts
    positions = jnp.arange(removed_count, dtype=jnp.int32)
    owners = jnp.sum((shard_ends[None, :] <= positions[:, None]).astype(jnp.int32), axis=1)
    shard_ids = jnp.arange(counts.shape[0], dtype=jnp.int32)
    owner_start = jnp.sum(jnp.where(owners[:, None] == shard_ids[None, :], shard_starts[None, :], 0), axis=1)
    return (owners * slot_count + positions - owner_start).astype(jnp.int32)

def reference(weight, eigenbasis, eigenvalues, removed_local, counts):
    shard_width = FF // N_COL
    flattened = (jnp.arange(N_COL, dtype=jnp.int32)[:, None] * shard_width + removed_local).reshape(-1)
    removed = jnp.take(flattened, compact_index(counts, K, KMAX), axis=0).astype(jnp.int32)
    chosen = jnp.take(eigenbasis, removed, axis=0).astype(jnp.float32)
    scaled = (chosen / eigenvalues[None, :]).astype(jnp.bfloat16)
    inverse_rows = lax.dot_general(scaled.astype(jnp.float32), eigenbasis.astype(jnp.float32), (((1,), (1,)), ((), ())), preferred_element_type=jnp.float32)
    block_matrix = jnp.take(inverse_rows, removed, axis=1)
    block_matrix = 0.5 * (block_matrix + block_matrix.T)
    factor = jnp.linalg.cholesky(block_matrix)
    targets = jnp.take(weight, removed, axis=1).astype(jnp.float32).T
    forward = lax.linalg.triangular_solve(factor, targets, left_side=True, lower=True)
    backward = lax.linalg.triangular_solve(factor, forward, left_side=True, lower=True, transpose_a=True)
    solved_half = backward.T.astype(jnp.bfloat16)
    rows_half = inverse_rows.astype(jnp.bfloat16)
    change = jnp.dot(solved_half.astype(jnp.float32), rows_half.astype(jnp.float32), preferred_element_type=jnp.float32)
    return (weight.astype(jnp.float32) - change).astype(jnp.bfloat16)
```

```python
import functools
import jax
import jax.numpy as jnp
from jax import lax
from jax.experimental import pallas as pl
from jax.experimental.pallas import tpu as pltpu
from jax.sharding import Mesh
from jax.sharding import PartitionSpec as P

KDEV = 24
COL = ("col_0", "col_1", "col_2")
ROW = ("row_0", "row_1")


def laid_out(parts, dim):
    dims = list(parts.shape[1:])
    dims[dim] *= parts.shape[0]
    return jnp.moveaxis(parts, 0, dim).reshape(dims)


def gather_in_order(array, axes, sequence):
    parts = array
    for k in sequence:
        parts = lax.all_gather(parts, axes[k])
    done = sequence[::-1]
    back = [done.index(k) for k in range(len(axes))]
    parts = parts.transpose(*back, *range(len(axes), parts.ndim))
    return parts.reshape(-1, *array.shape)


def whole_of(array, axes, sequence, dim):
    return laid_out(gather_in_order(array, axes, sequence), dim)


def split_up(array, dim, count):
    before, after = (array.shape[:dim], array.shape[dim + 1 :])
    return jnp.moveaxis(array.reshape(*before, count, -1, *after), dim, 0)


def sum_at_owner(array, axis, dim):
    parts = split_up(array, dim, lax.axis_size(axis))
    arrived = lax.all_to_all(parts, axis, split_axis=0, concat_axis=0, tiled=True)
    return arrived.sum(axis=0)


def from_everyone(array, axis):
    count = lax.axis_size(axis)
    return lax.all_to_all(
        jnp.broadcast_to(array[None], (count, *array.shape)), axis, 0, 0, tiled=True
    )


def gathered_copies(array, axis, dim):
    parts = from_everyone(array, axis)
    return laid_out(parts, dim)


def compact_index(counts, removed_count, slot_count):
    shard_ids = jnp.arange(counts.shape[0], dtype=jnp.int32)
    shard_starts = jnp.sum(jnp.where(shard_ids[None, :] < shard_ids[:, None], counts[None, :], 0), axis=1)
    shard_ends = shard_starts + counts
    positions = jnp.arange(removed_count, dtype=jnp.int32)
    owners = jnp.sum((shard_ends[None, :] <= positions[:, None]).astype(jnp.int32), axis=1)
    owner_start = jnp.sum(
        jnp.where(owners[:, None] == shard_ids[None, :], shard_starts[None, :], 0), axis=1
    )
    return owners * slot_count + positions - owner_start


HI = lax.Precision.HIGHEST
NB=128

def invert_block(block):
    lane = lax.broadcasted_iota(jnp.int32, (8, NB), 1)
    sub = lax.broadcasted_iota(jnp.int32, (8, NB), 0)
    tiles = [block[8 * i : 8 * i + 8, :] for i in range(NB // 8)]
    for b in range(NB // 8):
        here = (lane >= 8 * b) & (lane < 8 * b + 8)
        columns = [[jnp.broadcast_to(t[:, 8 * b + j : 8 * b + j + 1], (8, NB)) for j in range(8)] for t in tiles]
        pivots = list(columns[b])
        panel = jnp.where(here, jnp.where(lane - 8 * b == sub, 1.0, 0.0), tiles[b])
        for p in range(8):
            own = sub == p
            factor = pivots[p]
            inv = 1.0 / jnp.broadcast_to(factor[p : p + 1, :], (8, NB))
            def step(x):
                scaled = jnp.broadcast_to(x[p : p + 1, :], (8, NB)) * inv
                return jnp.where(own, scaled, x - factor * scaled)
            for q in range(p + 1, 8):
                pivots[q] = step(pivots[q])
            panel = step(panel)
        rows = [jnp.broadcast_to(panel[j : j + 1, :], (8, NB)) for j in range(8)]
        for i in range(NB // 8):
            if i == b:
                tiles[i] = panel
            else:
                t = jnp.where(here, 0.0, tiles[i])
                parts = [columns[i][j] * rows[j] for j in range(8)]
                while len(parts) > 1:
                    parts = [parts[2 * m] + parts[2 * m + 1] for m in range(len(parts) // 2)]
                tiles[i] = t - parts[0]
    return jnp.concatenate(tiles, axis=0)

def solve_kernel(nblk, matrix_ref, target_ref, out_ref, aug, upper, sol):
    width = nblk * NB
    for i in range(nblk):
        aug[i, :, :width] = matrix_ref[i * NB : (i + 1) * NB, :]
        aug[i, :, width:] = target_ref[i * NB : (i + 1) * NB, :].astype(jnp.float32)

    def eliminate(k, _):
        here = pl.ds(pl.multiple_of(k * NB, NB), NB)
        inverse = invert_block(aug[k, :, here])
        panel = jnp.dot(inverse, aug[k], preferred_element_type=jnp.float32, precision=HI)
        upper[k] = panel

        def update(i, _):
            there = pl.ds(pl.multiple_of(i * NB, NB), NB)
            aug[i] -= lax.dot_general(aug[k, :, there], upper[k], (((0,), (0,)), ((), ())),
                                      preferred_element_type=jnp.float32, precision=HI)
            return 0
        lax.fori_loop(k + 1, nblk, update, 0)
        return 0
    lax.fori_loop(0, nblk, eliminate, 0)
    for k in range(nblk - 1, -1, -1):
        x = upper[k, :, width:]
        if k < nblk - 1:
            x = x - jnp.dot(upper[k, :, (k + 1) * NB : width], sol[(k + 1) * NB :, :],
                            preferred_element_type=jnp.float32, precision=HI)
        sol[k * NB : (k + 1) * NB, :] = x
        out_ref[k * NB : (k + 1) * NB, :] = x.astype(jnp.bfloat16)

def solve(matrix, targets):
    k, d = targets.shape
    nblk = k // NB
    return pl.pallas_call(
        functools.partial(solve_kernel, nblk),
        out_shape=jax.ShapeDtypeStruct((k, d), jnp.bfloat16),
        in_specs=[pl.BlockSpec(memory_space=pltpu.VMEM)] * 2,
        out_specs=pl.BlockSpec(memory_space=pltpu.VMEM),
        scratch_shapes=[pltpu.VMEM((nblk, NB, k + d), jnp.float32), pltpu.VMEM((nblk, NB, k + d), jnp.float32),
                        pltpu.VMEM((k, d), jnp.float32)],
        compiler_params=pltpu.CompilerParams(vmem_limit_bytes=40 << 20),
    )(matrix, targets)


def shards(weight, eigenbasis, eigenvalues, removed_local, counts):
    removed_count = KDEV * lax.axis_size(COL)
    slot_count = removed_local.shape[1]
    local_picks = removed_local[0]
    compact_order = compact_index(counts, removed_count, slot_count)
    chosen = jnp.take(eigenbasis, local_picks, axis=0).astype(jnp.float32)
    scaled = (chosen / eigenvalues[None, :]).astype(jnp.bfloat16)
    gathered = whole_of(scaled, COL, (0, 1, 2), 0)
    compacted = jnp.take(gathered, compact_order, axis=0)
    partial_value = lax.dot_general(
        compacted, eigenbasis, (((1,), (1,)), ((), ())), preferred_element_type=jnp.float32
    )
    share = sum_at_owner(partial_value, ROW, 0)
    block_share = jnp.take(share, local_picks, axis=1)
    block_band = lax.all_gather(block_share, COL, axis=1, tiled=True)
    block_whole = whole_of(block_band, ROW, (0, 1), 0)
    share_half = share.astype(jnp.bfloat16)
    block_matrix = jnp.take(block_whole, compact_order, axis=1)
    block_matrix = 0.5 * (block_matrix + block_matrix.T)
    weight_piece = jnp.take(weight, local_picks, axis=1)
    everything = gathered_copies(weight_piece, COL, 1)
    everything = jnp.take(everything, compact_order, axis=1)
    solved_half = solve(block_matrix, everything.T)
    change = lax.dot_general(
        solved_half,
        lax.all_gather(share_half, ROW, axis=0, tiled=True),
        (((0,), (0,)), ((), ())),
        preferred_element_type=jnp.float32,
    )
    return (weight.astype(jnp.float32) - change).astype(jnp.bfloat16)


def solution(mesh):
    torus = Mesh(mesh.devices.reshape(2, 8, 2, 8, 2), ("row_0", "row_1", "col_0", "col_1", "col_2"))
    return jax.shard_map(
        shards,
        mesh=torus,
        in_specs=(P(ROW, COL), P(COL, ROW), P(ROW), P(COL, None), P()),
        out_specs=P(ROW, COL),
        check_vma=False,
    )
```

```python
import functools
import jax
import jax.numpy as jnp
from jax import lax
from jax.experimental import pallas as pl
from jax.experimental.pallas import tpu as pltpu
from jax.sharding import Mesh
from jax.sharding import PartitionSpec as P

KDEV = 24
COL = ("x_hi", "z", "core")
ROW = ("x_lo", "y")
MESH = pl.DeviceIdType.MESH
ROWS16 = 48


def laid_out(parts, dim):
    dims = list(parts.shape[1:])
    dims[dim] *= parts.shape[0]
    return jnp.moveaxis(parts, 0, dim).reshape(dims)


def gather_in_order(array, axes, sequence):
    parts = array
    for k in sequence:
        parts = lax.all_gather(parts, axes[k])
    done = sequence[::-1]
    back = [done.index(k) for k in range(len(axes))]
    parts = parts.transpose(*back, *range(len(axes), parts.ndim))
    return parts.reshape(-1, *array.shape)


def whole_of(array, axes, sequence, dim):
    return laid_out(gather_in_order(array, axes, sequence), dim)


def split_up(array, dim, count):
    before, after = (array.shape[:dim], array.shape[dim + 1 :])
    return jnp.moveaxis(array.reshape(*before, count, -1, *after), dim, 0)


def sum_at_owner(array, axis, dim):
    parts = split_up(array, dim, lax.axis_size(axis))
    arrived = lax.all_to_all(parts, axis, split_axis=0, concat_axis=0, tiled=True)
    return arrived.sum(axis=0)


def compact_index(counts, removed_count):
    shard_ids = jnp.arange(counts.shape[0], dtype=jnp.int32)
    shard_starts = jnp.sum(jnp.where(shard_ids[None, :] < shard_ids[:, None], counts[None, :], 0), axis=1)
    shard_ends = shard_starts + counts
    positions = jnp.arange(removed_count, dtype=jnp.int32)
    owners = jnp.sum((shard_ends[None, :] <= positions[:, None]).astype(jnp.int32), axis=1)
    owner_start = jnp.sum(
        jnp.where(owners[:, None] == shard_ids[None, :], shard_starts[None, :], 0), axis=1
    )
    return owners, positions - owner_start


HI = lax.Precision.HIGHEST
NB=128

def invert_block(block):
    lane = lax.broadcasted_iota(jnp.int32, (8, NB), 1)
    sub = lax.broadcasted_iota(jnp.int32, (8, NB), 0)
    tiles = [block[8 * i : 8 * i + 8, :] for i in range(NB // 8)]
    for b in range(NB // 8):
        here = (lane >= 8 * b) & (lane < 8 * b + 8)
        columns = [[jnp.broadcast_to(t[:, 8 * b + j : 8 * b + j + 1], (8, NB)) for j in range(8)] for t in tiles]
        pivots = list(columns[b])
        panel = jnp.where(here, jnp.where(lane - 8 * b == sub, 1.0, 0.0), tiles[b])
        for p in range(8):
            own = sub == p
            factor = pivots[p]
            inv = 1.0 / jnp.broadcast_to(factor[p : p + 1, :], (8, NB))
            def step(x):
                scaled = jnp.broadcast_to(x[p : p + 1, :], (8, NB)) * inv
                return jnp.where(own, scaled, x - factor * scaled)
            for q in range(p + 1, 8):
                pivots[q] = step(pivots[q])
            panel = step(panel)
        rows = [jnp.broadcast_to(panel[j : j + 1, :], (8, NB)) for j in range(8)]
        for i in range(NB // 8):
            if i == b:
                tiles[i] = panel
            else:
                t = jnp.where(here, 0.0, tiles[i])
                parts = [columns[i][j] * rows[j] for j in range(8)]
                while len(parts) > 1:
                    parts = [parts[2 * m] + parts[2 * m + 1] for m in range(len(parts) // 2)]
                tiles[i] = t - parts[0]
    return jnp.concatenate(tiles, axis=0)

def solve_kernel(nblk, matrix_ref, target_ref, out_ref, aug, upper, sol):
    width = nblk * NB
    for i in range(nblk):
        aug[i, :, :width] = matrix_ref[i * NB : (i + 1) * NB, :]
        aug[i, :, width:] = target_ref[i * NB : (i + 1) * NB, :].astype(jnp.float32)

    def eliminate(k, _):
        here = pl.ds(pl.multiple_of(k * NB, NB), NB)
        inverse = invert_block(aug[k, :, here])
        panel = jnp.dot(inverse, aug[k], preferred_element_type=jnp.float32, precision=HI)
        upper[k] = panel

        def update(i, _):
            there = pl.ds(pl.multiple_of(i * NB, NB), NB)
            aug[i] -= lax.dot_general(aug[k, :, there], upper[k], (((0,), (0,)), ((), ())),
                                      preferred_element_type=jnp.float32, precision=HI)
            return 0
        lax.fori_loop(k + 1, nblk, update, 0)
        return 0
    lax.fori_loop(0, nblk, eliminate, 0)
    for k in range(nblk - 1, -1, -1):
        x = upper[k, :, width:]
        if k < nblk - 1:
            x = x - jnp.dot(upper[k, :, (k + 1) * NB : width], sol[(k + 1) * NB :, :],
                            preferred_element_type=jnp.float32, precision=HI)
        sol[k * NB : (k + 1) * NB, :] = x
        out_ref[k * NB : (k + 1) * NB, :] = x.astype(jnp.bfloat16)

def solve(matrix, targets):
    k, d = targets.shape
    nblk = k // NB
    return pl.pallas_call(
        functools.partial(solve_kernel, nblk),
        out_shape=jax.ShapeDtypeStruct((k, d), jnp.bfloat16),
        in_specs=[pl.BlockSpec(memory_space=pltpu.VMEM)] * 2,
        out_specs=pl.BlockSpec(memory_space=pltpu.VMEM),
        scratch_shapes=[pltpu.VMEM((nblk, NB, k + d), jnp.float32), pltpu.VMEM((nblk, NB, k + d), jnp.float32),
                        pltpu.VMEM((k, d), jnp.float32)],
        compiler_params=pltpu.CompilerParams(vmem_limit_bytes=40 << 20),
    )(matrix, targets)


def remote(src, dst, sems, n, device):
    send, recv = sems
    return pltpu.make_async_remote_copy(
        src_ref=src, dst_ref=dst, send_sem=send.at[n], recv_sem=recv.at[n],
        device_id=device, device_id_type=MESH,
    )


def greet(devices):
    barrier = pltpu.get_barrier_semaphore()
    for device in devices:
        pl.semaphore_signal(barrier, inc=1, device_id=device, device_id_type=MESH)
    pl.semaphore_wait(barrier, len(devices))


class Gather:
    def __init__(self, source, out, sems, base, pair, ring, core, slot):
        self.source, self.out, self.sems, self.base = source, out, sems, base
        self.pair, self.ring, self.core, self.slot = pair, ring, core, slot
        self.p, self.r = lax.axis_index(pair), lax.axis_index(ring)
        self.k = lax.axis_index("core")
        self.n = lax.axis_size(ring)
        self.sent, self.number = [], {}

    @staticmethod
    def count(n, core):
        return 1 + 2 * (n - 1) + (2 * n if core else 0)

    def at(self, other, offset, sibling=False):
        p = 1 - self.p if other else self.p
        k = 1 - self.k if sibling else self.k
        return self.out.at[self.slot(p, lax.rem(self.r + offset + self.n, self.n), k)]

    def copy(self, name, src, dst, device):
        n = self.number.setdefault(name, len(self.number))
        return remote(src, dst, self.sems, self.base + n, device)

    def send(self, name, block, device):
        copy = self.copy(name, block[0], block[1], device)
        copy.start()
        self.sent.append(copy)

    def arrived(self, name, dst, device):
        self.copy(name, dst, dst, device).wait_recv()

    def step(self, way):
        return {self.ring: lax.rem(self.r + way + self.n, self.n)}

    def share(self, other, offset, block):
        if self.core:
            self.send(("core", other, offset % self.n), block, {"core": 1 - self.k})

    def begin(self):
        own = (self.source, self.at(False, 0))
        self.send("pair", own, {self.pair: 1 - self.p})
        for way in (1, -1):
            self.send((way, False, 1), own, self.step(way))
        self.share(False, 0, own)

    def spread_pair(self):
        block = self.at(True, 0)
        self.arrived("pair", block, {self.pair: 1 - self.p})
        for way in (1, -1):
            self.send((way, True, 1), (block, block), self.step(way))
        self.share(True, 0, (block, block))

    def advance(self, s):
        half = self.n // 2
        for other in (False, True):
            for way in (1, -1):
                last = half if (way == 1) != other else half - 1
                if s > last:
                    continue
                block = self.at(other, -way * s)
                self.arrived((way, other, s), block, self.step(way))
                if s < last:
                    self.send((way, other, s + 1), (block, block), self.step(way))
                self.share(other, -way * s, (block, block))

    def finish(self):
        if self.core:
            for other in (False, True):
                for offset in range(self.n):
                    self.arrived(("core", other, offset), self.at(other, offset, True), {"core": 1 - self.k})
        for copy in self.sent:
            copy.wait_send()

    def run(self):
        self.begin()
        self.spread_pair()
        for s in range(1, self.n // 2 + 1):
            self.advance(s)
        self.finish()


def col_slot(p, r, k):
    return (p * lax.axis_size("z") + r) * 2 + k


def row_slot(p, r, k):
    return p * lax.axis_size("y") + r


def col_neighbours():
    z, n = lax.axis_index("z"), lax.axis_size("z")
    return [
        {"core": 1 - lax.axis_index("core")},
        {"x_hi": 1 - lax.axis_index("x_hi")},
        {"z": lax.rem(z + 1, n)},
        {"z": lax.rem(z + n - 1, n)},
    ]


def gather_col_kernel(block_ref, out_ref, send, recv, local):
    mine = pltpu.make_async_copy(
        block_ref, out_ref.at[col_slot(lax.axis_index("x_hi"), lax.axis_index("z"), lax.axis_index("core"))], local
    )
    mine.start()
    greet(col_neighbours())
    Gather(block_ref, out_ref, (send, recv), 0, "x_hi", "z", True, col_slot).run()
    mine.wait()


def gather_col(block):
    n = Gather.count(lax.axis_size("z"), True)
    return pl.pallas_call(
        gather_col_kernel,
        out_shape=jax.ShapeDtypeStruct((lax.axis_size(COL), *block.shape), block.dtype),
        in_specs=[pl.BlockSpec(memory_space=pltpu.VMEM)],
        out_specs=pl.BlockSpec(memory_space=pltpu.VMEM),
        scratch_shapes=[pltpu.SemaphoreType.DMA((n,)), pltpu.SemaphoreType.DMA((n,)), pltpu.SemaphoreType.DMA],
        compiler_params=pltpu.CompilerParams(collective_id=0, has_side_effects=True, vmem_limit_bytes=40 << 20),
    )(block)


def picked(positions, size):
    return (positions[:, None] == jnp.arange(size, dtype=jnp.int32)[None, :]).astype(jnp.bfloat16)


def exact_rows(choice, array, dims):
    return lax.dot_general(choice, array, (dims, ((), ())), preferred_element_type=jnp.float32)


def payload_of(eigenbasis, weight, local_picks):
    slots, width = local_picks.shape[0], eigenbasis.shape[1]
    basis_rows = jnp.take(eigenbasis, local_picks, axis=0)
    columns = exact_rows(picked(local_picks, weight.shape[1]), weight, ((1,), (1,))).astype(jnp.bfloat16)
    columns = columns.reshape(ROWS16 - slots, -1)
    columns = jnp.pad(columns, ((0, 0), (0, width - columns.shape[1])))
    return jnp.concatenate([basis_rows, columns], axis=0)


def shards(weight, eigenbasis, eigenvalues, removed_local, counts):
    removed_count = KDEV * lax.axis_size(COL)
    slot_count = removed_local.shape[1]
    local_picks = removed_local[0]
    owners, ranks = compact_index(counts, removed_count)
    gathered = gather_col(payload_of(eigenbasis, weight, local_picks))
    shard_count, _, slab = gathered.shape
    basis = exact_rows(picked(owners * ROWS16 + ranks, shard_count * ROWS16), gathered.reshape(-1, slab), ((1,), (0,)))
    scaled = (basis / eigenvalues[None, :]).astype(jnp.bfloat16)
    columns = gathered[:, slot_count:, : slot_count // (ROWS16 - slot_count) * weight.shape[0]]
    targets = exact_rows(
        picked(owners * slot_count + ranks, shard_count * slot_count), columns.reshape(-1, weight.shape[0]), ((1,), (0,))
    ).astype(jnp.bfloat16)
    partial_value = lax.dot_general(
        scaled, eigenbasis, (((1,), (1,)), ((), ())), preferred_element_type=jnp.float32
    )
    share = sum_at_owner(partial_value, ROW, 0)
    block_share = jnp.take(share, local_picks, axis=1)
    block_band = lax.all_gather(block_share, COL, axis=1, tiled=True)
    block_whole = whole_of(block_band, ROW, (0, 1), 0)
    share_half = share.astype(jnp.bfloat16)
    block_matrix = jnp.take(block_whole, owners * slot_count + ranks, axis=1)
    block_matrix = 0.5 * (block_matrix + block_matrix.T)
    solved_half = solve(block_matrix, targets)
    change = lax.dot_general(
        solved_half,
        lax.all_gather(share_half, ROW, axis=0, tiled=True),
        (((0,), (0,)), ((), ())),
        preferred_element_type=jnp.float32,
    )
    return (weight.astype(jnp.float32) - change).astype(jnp.bfloat16)


def solution(mesh):
    torus = Mesh(mesh.devices.reshape(2, 8, 2, 8, 2), ("x_lo", "y", "x_hi", "z", "core"))
    return jax.shard_map(
        shards,
        mesh=torus,
        in_specs=(P(ROW, COL), P(COL, ROW), P(ROW), P(COL, None), P()),
        out_specs=P(ROW, COL),
        check_vma=False,
    )
```

```python
import functools
import jax
import jax.numpy as jnp
from jax import lax
from jax.experimental import pallas as pl
from jax.experimental.pallas import tpu as pltpu
from jax.sharding import Mesh
from jax.sharding import PartitionSpec as P

KDEV = 24
COL = ("x_hi", "z", "core")
ROW = ("x_lo", "y")
MESH = pl.DeviceIdType.MESH
ROWS16 = 48


def compact_index(counts, removed_count):
    shard_ids = jnp.arange(counts.shape[0], dtype=jnp.int32)
    shard_starts = jnp.sum(jnp.where(shard_ids[None, :] < shard_ids[:, None], counts[None, :], 0), axis=1)
    shard_ends = shard_starts + counts
    positions = jnp.arange(removed_count, dtype=jnp.int32)
    owners = jnp.sum((shard_ends[None, :] <= positions[:, None]).astype(jnp.int32), axis=1)
    owner_start = jnp.sum(
        jnp.where(owners[:, None] == shard_ids[None, :], shard_starts[None, :], 0), axis=1
    )
    return owners, positions - owner_start


HI = lax.Precision.HIGHEST
NB=128

def invert_block(block):
    lane = lax.broadcasted_iota(jnp.int32, (8, NB), 1)
    sub = lax.broadcasted_iota(jnp.int32, (8, NB), 0)
    tiles = [block[8 * i : 8 * i + 8, :] for i in range(NB // 8)]
    for b in range(NB // 8):
        here = (lane >= 8 * b) & (lane < 8 * b + 8)
        columns = [[jnp.broadcast_to(t[:, 8 * b + j : 8 * b + j + 1], (8, NB)) for j in range(8)] for t in tiles]
        pivots = list(columns[b])
        panel = jnp.where(here, jnp.where(lane - 8 * b == sub, 1.0, 0.0), tiles[b])
        for p in range(8):
            own = sub == p
            factor = pivots[p]
            inv = 1.0 / jnp.broadcast_to(factor[p : p + 1, :], (8, NB))
            def step(x):
                scaled = jnp.broadcast_to(x[p : p + 1, :], (8, NB)) * inv
                return jnp.where(own, scaled, x - factor * scaled)
            for q in range(p + 1, 8):
                pivots[q] = step(pivots[q])
            panel = step(panel)
        rows = [jnp.broadcast_to(panel[j : j + 1, :], (8, NB)) for j in range(8)]
        for i in range(NB // 8):
            if i == b:
                tiles[i] = panel
            else:
                t = jnp.where(here, 0.0, tiles[i])
                parts = [columns[i][j] * rows[j] for j in range(8)]
                while len(parts) > 1:
                    parts = [parts[2 * m] + parts[2 * m + 1] for m in range(len(parts) // 2)]
                tiles[i] = t - parts[0]
    return jnp.concatenate(tiles, axis=0)

def solve_kernel(nblk, matrix_ref, target_ref, out_ref, aug, upper, sol):
    width = nblk * NB
    for i in range(nblk):
        aug[i, :, :width] = matrix_ref[i * NB : (i + 1) * NB, :]
        aug[i, :, width:] = target_ref[i * NB : (i + 1) * NB, :].astype(jnp.float32)

    def eliminate(k, _):
        here = pl.ds(pl.multiple_of(k * NB, NB), NB)
        inverse = invert_block(aug[k, :, here])
        panel = jnp.dot(inverse, aug[k], preferred_element_type=jnp.float32, precision=HI)
        upper[k] = panel

        def update(i, _):
            there = pl.ds(pl.multiple_of(i * NB, NB), NB)
            aug[i] -= lax.dot_general(aug[k, :, there], upper[k], (((0,), (0,)), ((), ())),
                                      preferred_element_type=jnp.float32, precision=HI)
            return 0
        lax.fori_loop(k + 1, nblk, update, 0)
        return 0
    lax.fori_loop(0, nblk, eliminate, 0)
    for k in range(nblk - 1, -1, -1):
        x = upper[k, :, width:]
        if k < nblk - 1:
            x = x - jnp.dot(upper[k, :, (k + 1) * NB : width], sol[(k + 1) * NB :, :],
                            preferred_element_type=jnp.float32, precision=HI)
        sol[k * NB : (k + 1) * NB, :] = x
        out_ref[k * NB : (k + 1) * NB, :] = x.astype(jnp.bfloat16)

def solve(matrix, targets):
    k, d = targets.shape
    nblk = k // NB
    return pl.pallas_call(
        functools.partial(solve_kernel, nblk),
        out_shape=jax.ShapeDtypeStruct((k, d), jnp.bfloat16),
        in_specs=[pl.BlockSpec(memory_space=pltpu.VMEM)] * 2,
        out_specs=pl.BlockSpec(memory_space=pltpu.VMEM),
        scratch_shapes=[pltpu.VMEM((nblk, NB, k + d), jnp.float32), pltpu.VMEM((nblk, NB, k + d), jnp.float32),
                        pltpu.VMEM((k, d), jnp.float32)],
        compiler_params=pltpu.CompilerParams(vmem_limit_bytes=40 << 20),
    )(matrix, targets)


def remote(src, dst, sems, n, device):
    return pltpu.make_async_remote_copy(
        src_ref=src, dst_ref=dst, send_sem=sems[0].at[n], recv_sem=sems[1].at[n],
        device_id=device, device_id_type=MESH,
    )


def greet(devices):
    barrier = pltpu.get_barrier_semaphore()
    for device in devices:
        pl.semaphore_signal(barrier, inc=1, device_id=device, device_id_type=MESH)
    pl.semaphore_wait(barrier, len(devices))


class Gather:
    def __init__(self, source, out, sems, pair, ring, core, slot):
        self.source, self.out, self.sems = source, out, sems
        self.pair, self.ring, self.core, self.slot = pair, ring, core, slot
        self.p, self.r = lax.axis_index(pair), lax.axis_index(ring)
        self.k = lax.axis_index("core")
        self.n = lax.axis_size(ring)
        self.sent, self.number = [], {}

    @staticmethod
    def count(n, core):
        return 1 + 2 * (n - 1) + (2 * n if core else 0)

    def at(self, other, offset, sibling=False):
        p = 1 - self.p if other else self.p
        k = 1 - self.k if sibling else self.k
        return self.out.at[self.slot(p, lax.rem(self.r + offset + self.n, self.n), k)]

    def device(self, name):
        if name[0] == "pair":
            return {self.pair: 1 - self.p}
        if name[0] == "core":
            return {"core": 1 - self.k}
        return {self.ring: lax.rem(self.r + name[0] + self.n, self.n)}

    def copy(self, name, other, offset, own=False):
        block = self.at(other, offset)
        n = self.number.setdefault(name, len(self.number))
        return remote(self.source if own else block, block, self.sems, n, self.device(name))

    def send(self, *what):
        self.copy(*what).start()
        self.sent.append(what)

    def arrived(self, name, dst):
        remote(dst, dst, self.sems, self.number[name], self.device(name)).wait_recv()

    def share(self, other, offset, own=False):
        if self.core:
            self.send(("core", other, offset % self.n), other, offset, own)

    def begin(self):
        self.send(("pair",), False, 0, True)
        for way in (1, -1):
            self.send((way, False, 1), False, 0, True)
        self.share(False, 0, True)

    def spread_pair(self):
        self.arrived(("pair",), self.at(True, 0))
        for way in (1, -1):
            self.send((way, True, 1), True, 0)
        self.share(True, 0)

    def advance(self, s):
        half = self.n // 2
        for other in (False, True):
            for way in (1, -1):
                last = half if (way == 1) != other else half - 1
                if s > last:
                    continue
                self.arrived((way, other, s), self.at(other, -way * s))
                if s < last:
                    self.send((way, other, s + 1), other, -way * s)
                self.share(other, -way * s)

    def finish(self):
        if self.core:
            for other in (False, True):
                for offset in range(self.n):
                    self.arrived(("core", other, offset), self.at(other, offset, True))
        for what in self.sent:
            self.copy(*what).wait_send()

    def stages(self):
        rest = [functools.partial(self.advance, s) for s in range(1, self.n // 2 + 1)]
        return [self.begin, self.spread_pair, *rest, self.finish]


def col_slot(p, r, k):
    return (p * lax.axis_size("z") + r) * 2 + k


def row_slot(p, r, k):
    return p * lax.axis_size("y") + r


def col_neighbours():
    z, n = lax.axis_index("z"), lax.axis_size("z")
    return [
        {"core": 1 - lax.axis_index("core")},
        {"x_hi": 1 - lax.axis_index("x_hi")},
        {"z": lax.rem(z + 1, n)},
        {"z": lax.rem(z + n - 1, n)},
    ]


def col_here():
    return col_slot(lax.axis_index("x_hi"), lax.axis_index("z"), lax.axis_index("core"))


def dma_pair(*shape):
    return [pltpu.SemaphoreType.DMA(shape), pltpu.SemaphoreType.DMA(shape)]


def gather_col_kernel(block_ref, out_ref, send, recv, local):
    mine = pltpu.make_async_copy(block_ref, out_ref.at[col_here()], local)
    mine.start()
    greet(col_neighbours())
    for stage in Gather(block_ref, out_ref, (send, recv), "x_hi", "z", True, col_slot).stages():
        stage()
    mine.wait()


def gather_col(block):
    return pl.pallas_call(
        gather_col_kernel,
        out_shape=jax.ShapeDtypeStruct((lax.axis_size(COL), *block.shape), block.dtype),
        in_specs=[pl.BlockSpec(memory_space=pltpu.VMEM)],
        out_specs=pl.BlockSpec(memory_space=pltpu.VMEM),
        scratch_shapes=[*dma_pair(Gather.count(lax.axis_size("z"), True)), pltpu.SemaphoreType.DMA],
        compiler_params=pltpu.CompilerParams(collective_id=0, has_side_effects=True, vmem_limit_bytes=40 << 20),
    )(block)


class RowSum:
    def __init__(self, partial, ring_in, last_in, done, ring_sems, last_sems, parts):
        self.partial, self.ring_in, self.last_in, self.done = partial, ring_in, last_in, done
        self.ring_sems, self.last_sems = ring_sems, last_sems
        self.x, self.y, self.n = lax.axis_index("x_lo"), lax.axis_index("y"), lax.axis_size("y")
        rows = partial.shape[1] // parts
        self.cuts = [pl.ds(u * rows, rows) for u in range(parts)]

    def term(self, w, hops, u):
        way = 1 - 2 * w
        return self.partial.at[w * self.n + lax.rem(self.y - way * hops + 2 * self.n, self.n), self.cuts[u]]

    def copy(self, w, u, s):
        src = self.term(w, 1, u) if s == 0 else self.ring_in.at[w, s - 1, self.cuts[u]]
        n = (w * len(self.cuts) + u) * (self.n - 1) + s
        target = {"y": lax.rem(self.y + 1 - 2 * w + self.n, self.n)}
        return remote(src, self.ring_in.at[w, s, self.cuts[u]], self.ring_sems, n, target)

    def every(self):
        return [(w, u) for u in range(len(self.cuts)) for w in range(2)]

    def begin(self):
        for w, u in self.every():
            self.copy(w, u, 0).start()

    def advance(self, s):
        for w, u in self.every():
            self.copy(w, u, s).wait_recv()
            self.ring_in[w, s, self.cuts[u]] += self.term(w, 2 + s, u)[...]
            if s < self.n - 2:
                self.copy(w, u, s + 1).start()

    def last(self):
        return remote(self.ring_in.at[1 - self.x, self.n - 2], self.last_in, self.last_sems, 0, {"x_lo": 1 - self.x})

    def cross(self):
        self.last().start()

    def finish(self):
        self.last().wait_recv()
        self.done[row_slot(self.x, self.y, 0)] = (self.ring_in[self.x, self.n - 2] + self.last_in[...]).astype(jnp.bfloat16)
        for w, u in self.every():
            for s in range(self.n - 1):
                self.copy(w, u, s).wait_send()
        self.last().wait_send()

    def stages(self):
        return [self.begin, *[functools.partial(self.advance, s) for s in range(self.n - 1)], self.cross, self.finish]


class BandSum:
    def __init__(self, band, band_in, total, in_sems, out_sems):
        self.band, self.band_in, self.total = band, band_in, total
        self.in_sems, self.out_sems = in_sems, out_sems
        self.x, self.y, self.n = lax.axis_index("x_lo"), lax.axis_index("y"), lax.axis_size("y")
        self.bands = band.shape[1] // NB

    def peers(self):
        return [
            (lax.rem(self.x + dx, 2), lax.rem(self.y + dy, self.n))
            for dx in range(2) for dy in range(self.n) if dx or dy
        ]

    def home(self, p):
        return jnp.logical_and(self.x == p % 2, self.y == p)

    def inward(self, p, source):
        target = {"x_lo": jnp.int32(p % 2), "y": jnp.int32(p)}
        return pltpu.make_async_remote_copy(
            src_ref=self.band.at[:, pl.ds(p * NB, NB)], dst_ref=self.band_in.at[source],
            send_sem=self.in_sems[0].at[p], recv_sem=self.in_sems[1].at[source], device_id=target, device_id_type=MESH,
        )

    def outward(self, p, number, peer):
        cut = self.total.at[:, pl.ds(p * NB, NB)]
        return pltpu.make_async_remote_copy(
            src_ref=cut, dst_ref=cut, send_sem=self.out_sems[0].at[number], recv_sem=self.out_sems[1].at[p],
            device_id={"x_lo": peer[0], "y": peer[1]}, device_id_type=MESH,
        )

    def run(self):
        here = row_slot(self.x, self.y, 0)
        for p in range(self.bands):
            @pl.when(jnp.logical_not(self.home(p)))
            def _():
                self.inward(p, here).start()
        for p in range(self.bands):
            @pl.when(self.home(p))
            def _():
                total = self.band[:, p * NB : (p + 1) * NB]
                for x, y in self.peers():
                    source = row_slot(x, y, 0)
                    self.inward(p, source).wait_recv()
                    total = total + self.band_in[source]
                self.total[:, p * NB : (p + 1) * NB] = total
                for number, peer in enumerate(self.peers()):
                    self.outward(p, number, peer).start()
        for p in range(self.bands):
            @pl.when(jnp.logical_not(self.home(p)))
            def _():
                self.outward(p, 0, (jnp.int32(p % 2), jnp.int32(p))).wait_recv()

    def finish(self):
        here = row_slot(self.x, self.y, 0)
        for p in range(self.bands):
            @pl.when(jnp.logical_not(self.home(p)))
            def _():
                self.inward(p, here).wait_send()

            @pl.when(self.home(p))
            def _():
                for number, peer in enumerate(self.peers()):
                    self.outward(p, number, peer).wait_send()


def reduce_kernel(band_ref, partial_ref, matrix_ref, rows_ref, band_in, total, ring_in, last_in, *sems):
    pairs = [(sems[2 * i], sems[2 * i + 1]) for i in range(len(sems) // 2)]
    band = BandSum(band_ref, band_in, total, pairs[0], pairs[1])
    rows = RowSum(partial_ref, ring_in, last_in, rows_ref, pairs[2], pairs[3], 2)
    spread = Gather(total, matrix_ref, pairs[4], "x_hi", "z", True, col_slot)
    halves = Gather(rows_ref.at[row_slot(rows.x, rows.y, 0)], rows_ref, pairs[5], "x_lo", "y", False, row_slot)
    greet([{"x_lo": x, "y": y} for x, y in band.peers()] + col_neighbours())
    band.run()
    matrix_ref[col_here()] = total[...]
    first, second = spread.stages(), rows.stages() + halves.stages()
    for i in range(max(len(first), len(second))):
        if i < len(first):
            first[i]()
        if i < len(second):
            second[i]()
    band.finish()


def reduce_rows(band, partial):
    n, height, width = partial.shape
    ny, nz = lax.axis_size("y"), lax.axis_size("z")
    bands = band.shape[1] // NB
    return pl.pallas_call(
        reduce_kernel,
        out_shape=[
            jax.ShapeDtypeStruct((lax.axis_size(COL), *band.shape), jnp.float32),
            jax.ShapeDtypeStruct(partial.shape, jnp.bfloat16),
        ],
        in_specs=[pl.BlockSpec(memory_space=pltpu.VMEM)] * 2,
        out_specs=[pl.BlockSpec(memory_space=pltpu.VMEM)] * 2,
        scratch_shapes=[
            pltpu.VMEM((n, band.shape[0], NB), jnp.float32),
            pltpu.VMEM(band.shape, jnp.float32),
            pltpu.VMEM((2, ny - 1, height, width), jnp.float32),
            pltpu.VMEM((height, width), jnp.float32),
            pltpu.SemaphoreType.DMA((bands,)), pltpu.SemaphoreType.DMA((n,)),
            pltpu.SemaphoreType.DMA((n - 1,)), pltpu.SemaphoreType.DMA((bands,)),
            *dma_pair(4 * (ny - 1)), *dma_pair(1),
            *dma_pair(Gather.count(nz, True)), *dma_pair(Gather.count(ny, False)),
        ],
        compiler_params=pltpu.CompilerParams(collective_id=1, has_side_effects=True, vmem_limit_bytes=48 << 20),
    )(band, partial)


def picked(positions, size):
    return (positions[:, None] == jnp.arange(size, dtype=jnp.int32)[None, :]).astype(jnp.bfloat16)


def exact_rows(choice, array, dims):
    return lax.dot_general(choice, array, (dims, ((), ())), preferred_element_type=jnp.float32)


def payload_of(eigenbasis, weight, local_picks):
    slots, width = local_picks.shape[0], eigenbasis.shape[1]
    basis_rows = jnp.take(eigenbasis, local_picks, axis=0)
    columns = exact_rows(picked(local_picks, weight.shape[1]), weight, ((1,), (1,))).astype(jnp.bfloat16)
    columns = columns.reshape(ROWS16 - slots, -1)
    columns = jnp.pad(columns, ((0, 0), (0, width - columns.shape[1])))
    return jnp.concatenate([basis_rows, columns], axis=0)


def shards(weight, eigenbasis, eigenvalues, removed_local, counts):
    removed_count = KDEV * lax.axis_size(COL)
    slot_count = removed_local.shape[1]
    local_picks = removed_local[0]
    owners, ranks = compact_index(counts, removed_count)
    gathered = gather_col(payload_of(eigenbasis, weight, local_picks))
    shard_count, _, slab = gathered.shape
    compact = picked(owners * ROWS16 + ranks, shard_count * ROWS16)
    basis = exact_rows(compact, gathered.reshape(-1, slab), ((1,), (0,)))
    scaled = (basis / eigenvalues[None, :]).astype(jnp.bfloat16)
    basis = basis.astype(jnp.bfloat16)
    columns = gathered[:, slot_count:, : slot_count // (ROWS16 - slot_count) * weight.shape[0]]
    targets = exact_rows(
        picked(owners * slot_count + ranks, shard_count * slot_count), columns.reshape(-1, weight.shape[0]), ((1,), (0,))
    ).astype(jnp.bfloat16)
    first = lax.axis_index(COL) * KDEV
    band = exact_rows(lax.dynamic_slice_in_dim(scaled, first, KDEV), basis, ((1,), (1,)))
    band += exact_rows(lax.dynamic_slice_in_dim(basis, first, KDEV), scaled, ((1,), (1,)))
    partial = exact_rows(scaled, eigenbasis, ((1,), (1,)))
    row_count = lax.axis_size(ROW)
    matrix, rows = reduce_rows(0.5 * band, partial.reshape(row_count, -1, partial.shape[1]))
    solved_half = solve(matrix.reshape(removed_count, removed_count), targets)
    change = exact_rows(solved_half, rows.reshape(removed_count, -1), ((0,), (0,)))
    return (weight.astype(jnp.float32) - change).astype(jnp.bfloat16)


def solution(mesh):
    torus = Mesh(mesh.devices.reshape(2, 8, 2, 8, 2), ("x_lo", "y", "x_hi", "z", "core"))
    return jax.shard_map(
        shards,
        mesh=torus,
        in_specs=(P(ROW, COL), P(COL, ROW), P(ROW), P(COL, None), P()),
        out_specs=P(ROW, COL),
        check_vma=False,
    )
```

```python
import functools
import jax
import jax.numpy as jnp
from jax import lax
from jax.experimental import pallas as pl
from jax.experimental.pallas import tpu as pltpu
from jax.sharding import Mesh
from jax.sharding import PartitionSpec as P

KDEV = 24
COL = ("x_hi", "z", "core")
ROW = ("x_lo", "y")
MESH = pl.DeviceIdType.MESH
ROWS16 = 48


def compact_index(counts, removed_count):
    shard_ids = jnp.arange(counts.shape[0], dtype=jnp.int32)
    shard_starts = jnp.sum(jnp.where(shard_ids[None, :] < shard_ids[:, None], counts[None, :], 0), axis=1)
    shard_ends = shard_starts + counts
    positions = jnp.arange(removed_count, dtype=jnp.int32)
    owners = jnp.sum((shard_ends[None, :] <= positions[:, None]).astype(jnp.int32), axis=1)
    owner_start = jnp.sum(
        jnp.where(owners[:, None] == shard_ids[None, :], shard_starts[None, :], 0), axis=1
    )
    return owners, positions - owner_start


HI = lax.Precision.HIGHEST
NB=128

def invert_block(block):
    lane = lax.broadcasted_iota(jnp.int32, (8, NB), 1)
    sub = lax.broadcasted_iota(jnp.int32, (8, NB), 0)
    tiles = [block[8 * i : 8 * i + 8, :] for i in range(NB // 8)]
    for b in range(NB // 8):
        here = (lane >= 8 * b) & (lane < 8 * b + 8)
        columns = [[jnp.broadcast_to(t[:, 8 * b + j : 8 * b + j + 1], (8, NB)) for j in range(8)] for t in tiles]
        pivots = list(columns[b])
        panel = jnp.where(here, jnp.where(lane - 8 * b == sub, 1.0, 0.0), tiles[b])
        for p in range(8):
            own = sub == p
            factor = pivots[p]
            inv = 1.0 / jnp.broadcast_to(factor[p : p + 1, :], (8, NB))
            def step(x):
                scaled = jnp.broadcast_to(x[p : p + 1, :], (8, NB)) * inv
                return jnp.where(own, scaled, x - factor * scaled)
            for q in range(p + 1, 8):
                pivots[q] = step(pivots[q])
            panel = step(panel)
        rows = [jnp.broadcast_to(panel[j : j + 1, :], (8, NB)) for j in range(8)]
        for i in range(NB // 8):
            if i == b:
                tiles[i] = panel
            else:
                t = jnp.where(here, 0.0, tiles[i])
                parts = [columns[i][j] * rows[j] for j in range(8)]
                while len(parts) > 1:
                    parts = [parts[2 * m] + parts[2 * m + 1] for m in range(len(parts) // 2)]
                tiles[i] = t - parts[0]
    return jnp.concatenate(tiles, axis=0)

def load_system(count, matrix, targets, aug):
    width = count * NB
    for i in range(count):
        aug[i, :, :width] = matrix[i * NB : (i + 1) * NB, :]
        aug[i, :, width:] = targets[i * NB : (i + 1) * NB, :].astype(jnp.float32)


def solve_system(count, out, aug, upper, sol, beside):
    width = count * NB

    def pause(k, which):
        for i in range(count):
            if 2 * i + which < len(beside):
                @pl.when(k == i)
                def _():
                    for call in beside[2 * i + which]:
                        call()

    def eliminate(k, _):
        here = pl.ds(pl.multiple_of(k * NB, NB), NB)
        inverse = invert_block(aug[k, :, here])
        pause(k, 0)
        upper[k] = jnp.dot(inverse, aug[k], preferred_element_type=jnp.float32, precision=HI)

        def update(i, _):
            there = pl.ds(pl.multiple_of(i * NB, NB), NB)
            aug[i] -= lax.dot_general(
                aug[k, :, there], upper[k], (((0,), (0,)), ((), ())), preferred_element_type=jnp.float32, precision=HI
            )
            return 0

        lax.fori_loop(k + 1, count, update, 0)
        pause(k, 1)
        return 0

    lax.fori_loop(0, count, eliminate, 0)
    for k in range(count - 1, -1, -1):
        x = upper[k, :, width:]
        if k < count - 1:
            x = x - jnp.dot(
                upper[k, :, (k + 1) * NB : width], sol[(k + 1) * NB :, :],
                preferred_element_type=jnp.float32, precision=HI,
            )
        sol[k * NB : (k + 1) * NB, :] = x
        out[k * NB : (k + 1) * NB, :] = x.astype(jnp.bfloat16)


def remote(src, dst, sems, n, device):
    return pltpu.make_async_remote_copy(
        src_ref=src, dst_ref=dst, send_sem=sems[0].at[n], recv_sem=sems[1].at[n],
        device_id=device, device_id_type=MESH,
    )


def greet(devices):
    barrier = pltpu.get_barrier_semaphore()
    for device in devices:
        pl.semaphore_signal(barrier, inc=1, device_id=device, device_id_type=MESH)
    pl.semaphore_wait(barrier, len(devices))


class Gather:
    def __init__(self, source, out, sems, pair, ring, core, slot):
        self.source, self.out, self.sems = source, out, sems
        self.pair, self.ring, self.core, self.slot = pair, ring, core, slot
        self.p, self.r = lax.axis_index(pair), lax.axis_index(ring)
        self.k = lax.axis_index("core")
        self.n = lax.axis_size(ring)
        self.sends = self.plan()
        self.number = {what[0]: n for n, what in enumerate(self.sends)}

    def plan(self):
        half, sends = self.n // 2, []
        for other in (False, True):
            if not other:
                sends.append((("pair",), False, 0, True))
            for way in (1, -1):
                last = half if (way == 1) != other else half - 1
                for s in range(1, last + 1):
                    sends.append(((way, other, s), other, -way * (s - 1), not other and s == 1))
            if self.core:
                for offset in range(self.n):
                    sends.append((("core", other, offset), other, offset, not other and offset == 0))
        return sends

    @staticmethod
    def count(n, core):
        return 1 + 2 * (n - 1) + (2 * n if core else 0)

    def at(self, other, offset, sibling=False):
        p = 1 - self.p if other else self.p
        k = 1 - self.k if sibling else self.k
        return self.out.at[self.slot(p, lax.rem(self.r + offset + self.n, self.n), k)]

    def device(self, name):
        if name[0] == "pair":
            return {self.pair: 1 - self.p}
        if name[0] == "core":
            return {"core": 1 - self.k}
        return {self.ring: lax.rem(self.r + name[0] + self.n, self.n)}

    def copy(self, name, other, offset, own=False):
        block = self.at(other, offset)
        return remote(self.source if own else block, block, self.sems, self.number[name], self.device(name))

    def send(self, *what):
        self.copy(*what).start()

    def arrived(self, name, dst):
        remote(dst, dst, self.sems, self.number[name], self.device(name)).wait_recv()

    def share(self, other, offset, own=False):
        if self.core:
            self.send(("core", other, offset % self.n), other, offset, own)

    def begin(self):
        self.send(("pair",), False, 0, True)
        for way in (1, -1):
            self.send((way, False, 1), False, 0, True)
        self.share(False, 0, True)

    def spread_pair(self):
        self.arrived(("pair",), self.at(True, 0))
        for way in (1, -1):
            self.send((way, True, 1), True, 0)
        self.share(True, 0)

    def advance(self, s):
        half = self.n // 2
        for other in (False, True):
            for way in (1, -1):
                last = half if (way == 1) != other else half - 1
                if s > last:
                    continue
                self.arrived((way, other, s), self.at(other, -way * s))
                if s < last:
                    self.send((way, other, s + 1), other, -way * s)
                self.share(other, -way * s)

    def finish(self):
        if self.core:
            for other in (False, True):
                for offset in range(self.n):
                    self.arrived(("core", other, offset), self.at(other, offset, True))
        for what in self.sends:
            self.copy(*what).wait_send()

    def stages(self):
        rest = [functools.partial(self.advance, s) for s in range(1, self.n // 2 + 1)]
        return [self.begin, self.spread_pair, *rest, self.finish]


def col_slot(p, r, k):
    return (p * lax.axis_size("z") + r) * 2 + k


def row_slot(p, r, k):
    return p * lax.axis_size("y") + r


def col_neighbours():
    z, n = lax.axis_index("z"), lax.axis_size("z")
    return [
        {"core": 1 - lax.axis_index("core")},
        {"x_hi": 1 - lax.axis_index("x_hi")},
        {"z": lax.rem(z + 1, n)},
        {"z": lax.rem(z + n - 1, n)},
    ]


def col_here():
    return col_slot(lax.axis_index("x_hi"), lax.axis_index("z"), lax.axis_index("core"))


def dma_pair(*shape):
    return [pltpu.SemaphoreType.DMA(shape), pltpu.SemaphoreType.DMA(shape)]


def gather_col_kernel(block_ref, out_ref, send, recv, local):
    mine = pltpu.make_async_copy(block_ref, out_ref.at[col_here()], local)
    mine.start()
    greet(col_neighbours())
    for stage in Gather(block_ref, out_ref, (send, recv), "x_hi", "z", True, col_slot).stages():
        stage()
    mine.wait()


def gather_col(block):
    return pl.pallas_call(
        gather_col_kernel,
        out_shape=jax.ShapeDtypeStruct((lax.axis_size(COL), *block.shape), block.dtype),
        in_specs=[pl.BlockSpec(memory_space=pltpu.VMEM)],
        out_specs=pl.BlockSpec(memory_space=pltpu.VMEM),
        scratch_shapes=[*dma_pair(Gather.count(lax.axis_size("z"), True)), pltpu.SemaphoreType.DMA],
        compiler_params=pltpu.CompilerParams(collective_id=0, has_side_effects=True, vmem_limit_bytes=40 << 20),
    )(block)


class RowSum:
    def __init__(self, partial, ring_in, last_in, done, ring_sems, last_sems, parts):
        self.partial, self.ring_in, self.last_in, self.done = partial, ring_in, last_in, done
        self.ring_sems, self.last_sems = ring_sems, last_sems
        self.x, self.y, self.n = lax.axis_index("x_lo"), lax.axis_index("y"), lax.axis_size("y")
        rows = partial.shape[1] // parts
        self.cuts = [pl.ds(u * rows, rows) for u in range(parts)]

    def term(self, w, hops, u):
        way = 1 - 2 * w
        return self.partial.at[w * self.n + lax.rem(self.y - way * hops + 2 * self.n, self.n), self.cuts[u]]

    def copy(self, w, u, s):
        src = self.term(w, 1, u) if s == 0 else self.ring_in.at[w, s - 1, self.cuts[u]]
        n = (w * len(self.cuts) + u) * (self.n - 1) + s
        target = {"y": lax.rem(self.y + 1 - 2 * w + self.n, self.n)}
        return remote(src, self.ring_in.at[w, s, self.cuts[u]], self.ring_sems, n, target)

    def every(self):
        return [(w, u) for u in range(len(self.cuts)) for w in range(2)]

    def begin(self):
        for w, u in self.every():
            self.copy(w, u, 0).start()

    def advance(self, s):
        for w, u in self.every():
            self.copy(w, u, s).wait_recv()
            self.ring_in[w, s, self.cuts[u]] += self.term(w, 2 + s, u)[...]
            if s < self.n - 2:
                self.copy(w, u, s + 1).start()

    def last(self):
        return remote(self.ring_in.at[1 - self.x, self.n - 2], self.last_in, self.last_sems, 0, {"x_lo": 1 - self.x})

    def cross(self):
        self.last().start()

    def finish(self):
        self.last().wait_recv()
        self.done[row_slot(self.x, self.y, 0)] = (self.ring_in[self.x, self.n - 2] + self.last_in[...]).astype(jnp.bfloat16)
        for w, u in self.every():
            for s in range(self.n - 1):
                self.copy(w, u, s).wait_send()
        self.last().wait_send()

    def stages(self):
        return [self.begin, *[functools.partial(self.advance, s) for s in range(self.n - 1)], self.cross, self.finish]


class BandSum:
    def __init__(self, band, band_in, total, in_sems, out_sems):
        self.band, self.band_in, self.total = band, band_in, total
        self.in_sems, self.out_sems = in_sems, out_sems
        self.x, self.y, self.n = lax.axis_index("x_lo"), lax.axis_index("y"), lax.axis_size("y")
        self.bands = band.shape[1] // NB

    def peers(self):
        return [
            (lax.rem(self.x + dx, 2), lax.rem(self.y + dy, self.n))
            for dx in range(2) for dy in range(self.n) if dx or dy
        ]

    def home(self, p):
        return jnp.logical_and(self.x == p % 2, self.y == p)

    def inward(self, p, source):
        target = {"x_lo": jnp.int32(p % 2), "y": jnp.int32(p)}
        return pltpu.make_async_remote_copy(
            src_ref=self.band.at[:, pl.ds(p * NB, NB)], dst_ref=self.band_in.at[source],
            send_sem=self.in_sems[0].at[p], recv_sem=self.in_sems[1].at[source], device_id=target, device_id_type=MESH,
        )

    def outward(self, p, number, peer):
        cut = self.total.at[:, pl.ds(p * NB, NB)]
        return pltpu.make_async_remote_copy(
            src_ref=cut, dst_ref=cut, send_sem=self.out_sems[0].at[number], recv_sem=self.out_sems[1].at[p],
            device_id={"x_lo": peer[0], "y": peer[1]}, device_id_type=MESH,
        )

    def begin(self):
        here = row_slot(self.x, self.y, 0)
        for p in range(self.bands):
            @pl.when(jnp.logical_not(self.home(p)))
            def _():
                self.inward(p, here).start()

    def sum_home(self):
        for p in range(self.bands):
            @pl.when(self.home(p))
            def _():
                total = self.band[:, p * NB : (p + 1) * NB]
                for x, y in self.peers():
                    source = row_slot(x, y, 0)
                    self.inward(p, source).wait_recv()
                    total = total + self.band_in[source]
                self.total[:, p * NB : (p + 1) * NB] = total
                for number, peer in enumerate(self.peers()):
                    self.outward(p, number, peer).start()

    def arrive(self):
        for p in range(self.bands):
            @pl.when(jnp.logical_not(self.home(p)))
            def _():
                self.outward(p, 0, (jnp.int32(p % 2), jnp.int32(p))).wait_recv()

    def finish(self):
        here = row_slot(self.x, self.y, 0)
        for p in range(self.bands):
            @pl.when(jnp.logical_not(self.home(p)))
            def _():
                self.inward(p, here).wait_send()

            @pl.when(self.home(p))
            def _():
                for number, peer in enumerate(self.peers()):
                    self.outward(p, number, peer).wait_send()


def partial_rows(scaled, basis, partial, chunk):
    n, height, width = partial.shape
    calls = []
    for i in range(0, n, chunk):
        def call(i=i):
            value = lax.dot_general(
                scaled[i * height : (i + chunk) * height, :], basis[...], (((1,), (1,)), ((), ())),
                preferred_element_type=jnp.float32,
            )
            partial[i : i + chunk] = value.reshape(chunk, height, width)
        calls.append(call)
    return calls


def main_kernel(band_ref, scaled_ref, basis_ref, target_ref, solved_ref, rows_ref, band_in, total, partial, matrix,
                ring_in, last_in, aug, upper, sol, *sems):
    pairs = [(sems[2 * i], sems[2 * i + 1]) for i in range(len(sems) // 2)]
    band = BandSum(band_ref, band_in, total, pairs[0], pairs[1])
    rows = RowSum(partial, ring_in, last_in, rows_ref, pairs[2], pairs[3], 2)
    spread = Gather(total, matrix, pairs[4], "x_hi", "z", True, col_slot)
    halves = Gather(rows_ref.at[row_slot(rows.x, rows.y, 0)], rows_ref, pairs[5], "x_lo", "y", False, row_slot)
    greet([{"x_lo": x, "y": y} for x, y in band.peers()] + col_neighbours())
    products = partial_rows(scaled_ref, basis_ref, partial, 4)
    band.begin()
    products[0]()
    products[1]()
    band.sum_home()
    products[2]()
    products[3]()
    band.arrive()
    first, rest = spread.stages(), rows.stages() + halves.stages()
    first.pop(0)()
    rest.pop(0)()
    matrix[col_here()] = total[...]
    for i, stage in enumerate(first):
        stage()
        if i in (1, 3):
            rest.pop(0)()
    count = solved_ref.shape[0] // NB
    load_system(count, matrix.reshape(count * NB, count * NB), target_ref, aug)
    beside = [[stage] for stage in rest[: 2 * count]]
    solve_system(count, solved_ref, aug, upper, sol, beside)
    for stage in rest[2 * count :]:
        stage()
    band.finish()


def update_factors(band, scaled, basis, targets):
    n, ny, nz = lax.axis_size(ROW), lax.axis_size("y"), lax.axis_size("z")
    count, width = targets.shape
    height = count // n
    bands, blocks = band.shape[1] // NB, count // NB
    return pl.pallas_call(
        main_kernel,
        out_shape=[
            jax.ShapeDtypeStruct(targets.shape, jnp.bfloat16),
            jax.ShapeDtypeStruct((n, height, basis.shape[0]), jnp.bfloat16),
        ],
        in_specs=[pl.BlockSpec(memory_space=pltpu.VMEM)] * 4,
        out_specs=[pl.BlockSpec(memory_space=pltpu.VMEM)] * 2,
        scratch_shapes=[
            pltpu.VMEM((n, band.shape[0], NB), jnp.float32),
            pltpu.VMEM(band.shape, jnp.float32),
            pltpu.VMEM((n, height, basis.shape[0]), jnp.float32),
            pltpu.VMEM((lax.axis_size(COL), *band.shape), jnp.float32),
            pltpu.VMEM((2, ny - 1, height, basis.shape[0]), jnp.float32),
            pltpu.VMEM((height, basis.shape[0]), jnp.float32),
            pltpu.VMEM((blocks, NB, count + width), jnp.float32),
            pltpu.VMEM((blocks, NB, count + width), jnp.float32),
            pltpu.VMEM(targets.shape, jnp.float32),
            pltpu.SemaphoreType.DMA((bands,)), pltpu.SemaphoreType.DMA((n,)),
            pltpu.SemaphoreType.DMA((n - 1,)), pltpu.SemaphoreType.DMA((bands,)),
            *dma_pair(4 * (ny - 1)), *dma_pair(1),
            *dma_pair(Gather.count(nz, True)), *dma_pair(Gather.count(ny, False)),
        ],
        compiler_params=pltpu.CompilerParams(collective_id=1, has_side_effects=True, vmem_limit_bytes=56 << 20),
    )(band, scaled, basis, targets)


def picked(positions, size):
    return (positions[:, None] == jnp.arange(size, dtype=jnp.int32)[None, :]).astype(jnp.bfloat16)


def exact_rows(choice, array, dims):
    return lax.dot_general(choice, array, (dims, ((), ())), preferred_element_type=jnp.float32)


def payload_of(eigenbasis, weight, local_picks):
    slots, width = local_picks.shape[0], eigenbasis.shape[1]
    basis_rows = jnp.take(eigenbasis, local_picks, axis=0)
    columns = exact_rows(picked(local_picks, weight.shape[1]), weight, ((1,), (1,))).astype(jnp.bfloat16)
    columns = columns.reshape(ROWS16 - slots, -1)
    columns = jnp.pad(columns, ((0, 0), (0, width - columns.shape[1])))
    return jnp.concatenate([basis_rows, columns], axis=0)


def shards(weight, eigenbasis, eigenvalues, removed_local, counts):
    removed_count = KDEV * lax.axis_size(COL)
    slot_count = removed_local.shape[1]
    local_picks = removed_local[0]
    owners, ranks = compact_index(counts, removed_count)
    gathered = gather_col(payload_of(eigenbasis, weight, local_picks))
    shard_count, _, slab = gathered.shape
    compact = picked(owners * ROWS16 + ranks, shard_count * ROWS16)
    basis = exact_rows(compact, gathered.reshape(-1, slab), ((1,), (0,)))
    scaled = (basis / eigenvalues[None, :]).astype(jnp.bfloat16)
    basis = basis.astype(jnp.bfloat16)
    columns = gathered[:, slot_count:, : slot_count // (ROWS16 - slot_count) * weight.shape[0]]
    targets = exact_rows(
        picked(owners * slot_count + ranks, shard_count * slot_count), columns.reshape(-1, weight.shape[0]), ((1,), (0,))
    ).astype(jnp.bfloat16)
    first = lax.axis_index(COL) * KDEV
    band = exact_rows(lax.dynamic_slice_in_dim(scaled, first, KDEV), basis, ((1,), (1,)))
    band += exact_rows(lax.dynamic_slice_in_dim(basis, first, KDEV), scaled, ((1,), (1,)))
    solved_half, rows = update_factors(0.5 * band, scaled, eigenbasis, targets)
    change = exact_rows(solved_half, rows.reshape(removed_count, -1), ((0,), (0,)))
    return (weight.astype(jnp.float32) - change).astype(jnp.bfloat16)


def solution(mesh):
    torus = Mesh(mesh.devices.reshape(2, 8, 2, 8, 2), ("x_lo", "y", "x_hi", "z", "core"))
    return jax.shard_map(
        shards,
        mesh=torus,
        in_specs=(P(ROW, COL), P(COL, ROW), P(ROW), P(COL, None), P()),
        out_specs=P(ROW, COL),
        check_vma=False,
    )
```

```python
import functools
import jax
import jax.numpy as jnp
from jax import lax
from jax.experimental import pallas as pl
from jax.experimental.pallas import tpu as pltpu
from jax.sharding import Mesh
from jax.sharding import PartitionSpec as P

KDEV = 24
COL = ("x_hi", "z", "core")
ROW = ("x_lo", "y")
MESH = pl.DeviceIdType.MESH
ROWS16 = 48


def compact_index(counts, removed_count):
    shard_ids = jnp.arange(counts.shape[0], dtype=jnp.int32)
    shard_starts = jnp.sum(jnp.where(shard_ids[None, :] < shard_ids[:, None], counts[None, :], 0), axis=1)
    shard_ends = shard_starts + counts
    positions = jnp.arange(removed_count, dtype=jnp.int32)
    owners = jnp.sum((shard_ends[None, :] <= positions[:, None]).astype(jnp.int32), axis=1)
    owner_start = jnp.sum(
        jnp.where(owners[:, None] == shard_ids[None, :], shard_starts[None, :], 0), axis=1
    )
    return owners, positions - owner_start


HI = lax.Precision.HIGHEST
NB = 128
PAUSES = (4, 9)
BREAKS = len(PAUSES) + 2
PARTS = 3
EARLY = (0, 0, 1, 2, 2, 2, 2, 2, 0)

def lane_spread(tile, lane):
    return jnp.broadcast_to(tile[:, lane : lane + 1], tile.shape)


def invert_block(block, pause):
    lane = lax.broadcasted_iota(jnp.int32, (8, NB), 1)
    sub = lax.broadcasted_iota(jnp.int32, (8, NB), 0)
    count = NB // 8
    tiles = [block[8 * i : 8 * i + 8, :] for i in range(count)]
    for b in range(count):
        here = (lane >= 8 * b) & (lane < 8 * b + 8)
        pivots = [lane_spread(tiles[b], 8 * b + j) for j in range(8)]
        panel = jnp.where(here, jnp.where(lane - 8 * b == sub, 1.0, 0.0), tiles[b])
        for p in range(8):
            own = sub == p
            factor = pivots[p]
            inv = 1.0 / jnp.broadcast_to(factor[p : p + 1, :], (8, NB))

            def step(x):
                scaled = jnp.broadcast_to(x[p : p + 1, :], (8, NB)) * inv
                return jnp.where(own, scaled, x - factor * scaled)

            for q in range(p + 1, 8):
                pivots[q] = step(pivots[q])
            panel = step(panel)
        if b < count - 1:
            parts = [
                lane_spread(tiles[b + 1], 8 * b + j) * jnp.broadcast_to(panel[j : j + 1, :], (8, NB)) for j in range(8)
            ]
            while len(parts) > 1:
                parts = [parts[2 * m] + parts[2 * m + 1] for m in range(len(parts) // 2)]
            following = jnp.where(here, 0.0, tiles[b + 1]) - parts[0]
        spread = [panel]
        if b:
            spread.insert(0, jnp.zeros((8 * b, NB), jnp.float32))
        if b < count - 1:
            spread.append(jnp.zeros((NB - 8 * b - 8, NB), jnp.float32))
        change = jnp.dot(
            jnp.concatenate(tiles, axis=0), jnp.concatenate(spread, axis=0),
            preferred_element_type=jnp.float32, precision=HI,
        )
        for i in range(count):
            if i == b:
                tiles[i] = panel
            elif i == b + 1:
                tiles[i] = following
            else:
                tiles[i] = jnp.where(here, 0.0, tiles[i]) - change[8 * i : 8 * i + 8, :]
        if b in PAUSES:
            pause(PAUSES.index(b))
    return jnp.concatenate(tiles, axis=0)


def load_system(count, matrix, targets, aug):
    width = count * NB
    for i in range(count):
        aug[i, :, :width] = matrix[i * NB : (i + 1) * NB, :]
        aug[i, :, width:] = targets[i * NB : (i + 1) * NB, :].astype(jnp.float32)


def solve_system(count, out, aug, upper, sol, beside):
    width = count * NB

    def pause(k, which):
        for i in range(count):
            stages = beside[BREAKS * i + which]
            if stages:
                @pl.when(k == i)
                def _():
                    for stage in stages:
                        stage()

    def eliminate(k, _):
        here = pl.ds(pl.multiple_of(k * NB, NB), NB)
        inverse = invert_block(aug[k, :, here], functools.partial(pause, k))
        pause(k, BREAKS - 2)
        upper[k] = jnp.dot(inverse, aug[k], preferred_element_type=jnp.float32, precision=HI)

        def update(i, _):
            there = pl.ds(pl.multiple_of(i * NB, NB), NB)
            aug[i] -= lax.dot_general(
                aug[k, :, there], upper[k], (((0,), (0,)), ((), ())), preferred_element_type=jnp.float32, precision=HI
            )
            return 0

        lax.fori_loop(k + 1, count, update, 0)
        pause(k, BREAKS - 1)
        return 0

    lax.fori_loop(0, count, eliminate, 0)
    for k in range(count - 1, -1, -1):
        x = upper[k, :, width:]
        if k < count - 1:
            x = x - jnp.dot(
                upper[k, :, (k + 1) * NB : width], sol[(k + 1) * NB :, :],
                preferred_element_type=jnp.float32, precision=HI,
            )
        sol[k * NB : (k + 1) * NB, :] = x
        out[k * NB : (k + 1) * NB, :] = x.astype(jnp.bfloat16)


def remote(src, dst, sems, n, device):
    return pltpu.make_async_remote_copy(
        src_ref=src, dst_ref=dst, send_sem=sems[0].at[n], recv_sem=sems[1].at[n],
        device_id=device, device_id_type=MESH,
    )


def greet(devices):
    barrier = pltpu.get_barrier_semaphore()
    for device in devices:
        pl.semaphore_signal(barrier, inc=1, device_id=device, device_id_type=MESH)
    pl.semaphore_wait(barrier, len(devices))


class Gather:
    def __init__(self, source, out, sems, pair, ring, core, slot, near=0, cuts=None):
        self.source, self.out, self.sems = source, out, sems
        self.pair, self.ring, self.core, self.slot = pair, ring, core, slot
        self.near = near
        self.cuts = cuts or [pl.ds(0, source.shape[0])]
        self.p, self.r = lax.axis_index(pair), lax.axis_index(ring)
        self.k = lax.axis_index("core")
        self.n = lax.axis_size(ring)
        self.sends = self.plan()
        self.number = {what[0]: n for n, what in enumerate(self.sends)}

    def last(self, other, way):
        return self.n // 2 if (way == 1) != other else self.n // 2 - 1

    def plan(self):
        sends = []
        for u in range(len(self.cuts)):
            sends.append((("pair", u, 1, 0), False, 0, True))
            for way in (1, -1):
                for s in range(1, self.near + 1):
                    sends.append((("pair", u, way, s), False, -way * s, False))
                for s in range(1, self.last(False, way) + 1):
                    sends.append(((way, u, False, s), False, -way * (s - 1), s == 1))
                for s in range(self.near + 1, self.last(True, way) + 1):
                    sends.append(((way, u, True, s), True, -way * (s - 1), False))
            if self.core:
                for other in (False, True):
                    for offset in range(self.n):
                        sends.append((("core", u, other, offset), other, offset, not other and offset == 0))
        return sends

    @staticmethod
    def count(n, core, near=0, parts=1):
        return parts * (1 + 2 * near + (n - 1) + (n - 1 - 2 * near) + (2 * n if core else 0))

    def at(self, u, other, offset, sibling=False):
        p = 1 - self.p if other else self.p
        k = 1 - self.k if sibling else self.k
        return self.out.at[self.slot(p, lax.rem(self.r + offset + self.n, self.n), k), self.cuts[u]]

    def device(self, name):
        if name[0] == "pair":
            return {self.pair: 1 - self.p}
        if name[0] == "core":
            return {"core": 1 - self.k}
        return {self.ring: lax.rem(self.r + name[0] + self.n, self.n)}

    def copy(self, name):
        n = self.number[name]
        _, other, offset, own = self.sends[n]
        block = self.at(name[1], other, offset)
        return remote(self.source.at[self.cuts[name[1]]] if own else block, block, self.sems, n, self.device(name))

    def send(self, *name):
        self.copy(name).start()

    def arrived(self, dst, *name):
        remote(dst, dst, self.sems, self.number[name], self.device(name)).wait_recv()

    def share(self, u, other, offset):
        if self.core:
            self.send("core", u, other, offset % self.n)

    def begin(self, u):
        self.send("pair", u, 1, 0)
        for way in (1, -1):
            self.send(way, u, False, 1)
        self.share(u, False, 0)

    def cross(self, s, u):
        for way in (1, -1) if s else (1,):
            self.arrived(self.at(u, True, -way * s), "pair", u, way, s)
            for onward in (way,) if s else (1, -1):
                if s == self.near and s < self.last(True, onward):
                    self.send(onward, u, True, s + 1)
            self.share(u, True, -way * s)

    def advance(self, other, s, u):
        for way in (1, -1):
            if s > self.last(other, way):
                continue
            self.arrived(self.at(u, other, -way * s), way, u, other, s)
            if s < self.last(other, way):
                self.send(way, u, other, s + 1)
            if not other and s <= self.near:
                self.send("pair", u, way, s)
            self.share(u, other, -way * s)

    def finish(self):
        for u in range(len(self.cuts)):
            if self.core:
                for other in (False, True):
                    for offset in range(self.n):
                        self.arrived(self.at(u, other, offset, True), "core", u, other, offset)
        for what in self.sends:
            self.copy(what[0]).wait_send()

    def stages(self):
        own = [functools.partial(self.advance, False, s) for s in range(1, self.n // 2 + 1)]
        pair = [functools.partial(self.cross, s) for s in range(self.near + 1)]
        pair += [functools.partial(self.advance, True, s) for s in range(self.near + 1, self.n // 2 + 1)]
        mixed = [stage for both in zip(own, pair) for stage in both] + pair[len(own):]

        def each(stage):
            for u in range(len(self.cuts)):
                stage(u)

        return [functools.partial(each, stage) for stage in [self.begin, *mixed]] + [self.finish]


def col_slot(p, r, k):
    return (p * lax.axis_size("z") + r) * 2 + k


def row_slot(p, r, k):
    return p * lax.axis_size("y") + r


def col_neighbours():
    z, n = lax.axis_index("z"), lax.axis_size("z")
    return [
        {"core": 1 - lax.axis_index("core")},
        {"x_hi": 1 - lax.axis_index("x_hi")},
        {"z": lax.rem(z + 1, n)},
        {"z": lax.rem(z + n - 1, n)},
    ]


def col_here():
    return col_slot(lax.axis_index("x_hi"), lax.axis_index("z"), lax.axis_index("core"))


def row_cuts(ref, parts):
    rows = ref.shape[0] // parts
    return [pl.ds(u * rows, rows) for u in range(parts)]


def dma_pair(*shape):
    return [pltpu.SemaphoreType.DMA(shape), pltpu.SemaphoreType.DMA(shape)]


def gather_col_kernel(block_ref, out_ref, send, recv, local):
    mine = pltpu.make_async_copy(block_ref, out_ref.at[col_here()], local)
    mine.start()
    greet(col_neighbours())
    gather = Gather(block_ref, out_ref, (send, recv), "x_hi", "z", True, col_slot, 1, row_cuts(block_ref, PARTS))
    for stage in gather.stages():
        stage()
    mine.wait()


def gather_col(block):
    return pl.pallas_call(
        gather_col_kernel,
        out_shape=jax.ShapeDtypeStruct((lax.axis_size(COL), *block.shape), block.dtype),
        in_specs=[pl.BlockSpec(memory_space=pltpu.VMEM)],
        out_specs=pl.BlockSpec(memory_space=pltpu.VMEM),
        scratch_shapes=[*dma_pair(Gather.count(lax.axis_size("z"), True, 1, PARTS)), pltpu.SemaphoreType.DMA],
        compiler_params=pltpu.CompilerParams(collective_id=0, has_side_effects=True, vmem_limit_bytes=40 << 20),
    )(block)


class RowSum:
    def __init__(self, partial, ring_in, last_in, done, ring_sems, last_sems, parts):
        self.partial, self.ring_in, self.last_in, self.done = partial, ring_in, last_in, done
        self.ring_sems, self.last_sems = ring_sems, last_sems
        self.x, self.y, self.n = lax.axis_index("x_lo"), lax.axis_index("y"), lax.axis_size("y")
        rows = partial.shape[1] // parts
        self.cuts = [pl.ds(u * rows, rows) for u in range(parts)]

    def term(self, w, hops, u):
        way = 1 - 2 * w
        return self.partial.at[w * self.n + lax.rem(self.y - way * hops + 2 * self.n, self.n), self.cuts[u]]

    def copy(self, w, u, s):
        src = self.term(w, 1, u) if s == 0 else self.ring_in.at[w, s - 1, self.cuts[u]]
        n = (w * len(self.cuts) + u) * (self.n - 1) + s
        target = {"y": lax.rem(self.y + 1 - 2 * w + self.n, self.n)}
        return remote(src, self.ring_in.at[w, s, self.cuts[u]], self.ring_sems, n, target)

    def every(self):
        return [(w, u) for u in range(len(self.cuts)) for w in range(2)]

    def begin(self):
        for w, u in self.every():
            self.copy(w, u, 0).start()

    def advance(self, s, u):
        for w in range(2):
            self.copy(w, u, s).wait_recv()
            self.ring_in[w, s, self.cuts[u]] += self.term(w, 2 + s, u)[...]
            if s < self.n - 2:
                self.copy(w, u, s + 1).start()

    def last(self, u):
        src = self.ring_in.at[1 - self.x, self.n - 2, self.cuts[u]]
        return remote(src, self.last_in.at[self.cuts[u]], self.last_sems, u, {"x_lo": 1 - self.x})

    def cross(self, u):
        self.last(u).start()

    def round(self, u):
        self.last(u).wait_recv()
        value = self.ring_in[self.x, self.n - 2, self.cuts[u]] + self.last_in[self.cuts[u]]
        self.done[row_slot(self.x, self.y, 0), self.cuts[u]] = value.astype(jnp.bfloat16)

    def finish(self):
        for w, u in self.every():
            for s in range(self.n - 1):
                self.copy(w, u, s).wait_send()
        for u in range(len(self.cuts)):
            self.last(u).wait_send()

    def steps(self):
        return [functools.partial(self.advance, s, u) for s in range(self.n - 1) for u in range(len(self.cuts))]


class BandSum:
    def __init__(self, band, band_in, total, in_sems, out_sems):
        self.band, self.band_in, self.total = band, band_in, total
        self.in_sems, self.out_sems = in_sems, out_sems
        self.x, self.y, self.n = lax.axis_index("x_lo"), lax.axis_index("y"), lax.axis_size("y")
        self.bands = band.shape[1] // NB

    def peers(self):
        return [
            (lax.rem(self.x + dx, 2), lax.rem(self.y + dy, self.n))
            for dx in range(2) for dy in range(self.n) if dx or dy
        ]

    def home(self, p):
        return jnp.logical_and(self.x == p % 2, self.y == p)

    def inward(self, p, source):
        target = {"x_lo": jnp.int32(p % 2), "y": jnp.int32(p)}
        return pltpu.make_async_remote_copy(
            src_ref=self.band.at[:, pl.ds(p * NB, NB)], dst_ref=self.band_in.at[source],
            send_sem=self.in_sems[0].at[p], recv_sem=self.in_sems[1].at[source], device_id=target, device_id_type=MESH,
        )

    def outward(self, p, number, peer):
        cut = self.total.at[:, pl.ds(p * NB, NB)]
        return pltpu.make_async_remote_copy(
            src_ref=cut, dst_ref=cut, send_sem=self.out_sems[0].at[number], recv_sem=self.out_sems[1].at[p],
            device_id={"x_lo": peer[0], "y": peer[1]}, device_id_type=MESH,
        )

    def begin(self):
        here = row_slot(self.x, self.y, 0)
        for p in range(self.bands):
            @pl.when(jnp.logical_not(self.home(p)))
            def _():
                self.inward(p, here).start()

    def sum_home(self):
        for p in range(self.bands):
            @pl.when(self.home(p))
            def _():
                total = self.band[:, p * NB : (p + 1) * NB]
                for x, y in self.peers():
                    source = row_slot(x, y, 0)
                    self.inward(p, source).wait_recv()
                    total = total + self.band_in[source]
                self.total[:, p * NB : (p + 1) * NB] = total
                for number, peer in enumerate(self.peers()):
                    self.outward(p, number, peer).start()

    def arrive(self):
        for p in range(self.bands):
            @pl.when(jnp.logical_not(self.home(p)))
            def _():
                self.outward(p, 0, (jnp.int32(p % 2), jnp.int32(p))).wait_recv()

    def finish(self):
        here = row_slot(self.x, self.y, 0)
        for p in range(self.bands):
            @pl.when(jnp.logical_not(self.home(p)))
            def _():
                self.inward(p, here).wait_send()

            @pl.when(self.home(p))
            def _():
                for number, peer in enumerate(self.peers()):
                    self.outward(p, number, peer).wait_send()


def partial_rows(scaled, basis, partial, chunk):
    n, height, width = partial.shape
    calls = []
    for i in range(0, n, chunk):
        def call(i=i):
            value = lax.dot_general(
                scaled[i * height : (i + chunk) * height, :], basis[...], (((1,), (1,)), ((), ())),
                preferred_element_type=jnp.float32,
            )
            partial[i : i + chunk] = value.reshape(chunk, height, width)
        calls.append(call)
    return calls


def main_kernel(band_ref, scaled_ref, basis_ref, target_ref, solved_ref, rows_ref, band_in, total, partial, matrix,
                ring_in, last_in, aug, upper, sol, *sems):
    pairs = [(sems[2 * i], sems[2 * i + 1]) for i in range(len(sems) // 2)]
    band = BandSum(band_ref, band_in, total, pairs[0], pairs[1])
    rows = RowSum(partial, ring_in, last_in, rows_ref, pairs[2], pairs[3], PARTS)
    spread = Gather(total, matrix, pairs[4], "x_hi", "z", True, col_slot, 1, row_cuts(total, PARTS))
    own_rows = rows_ref.at[row_slot(rows.x, rows.y, 0)]
    halves = Gather(own_rows, rows_ref, pairs[5], "x_lo", "y", False, row_slot, 1, row_cuts(own_rows, PARTS))
    greet([{"x_lo": x, "y": y} for x, y in band.peers()] + col_neighbours())
    products = partial_rows(scaled_ref, basis_ref, partial, 4)
    band.begin()
    band.sum_home()
    band.arrive()
    first, rest = spread.stages(), rows.steps()
    for u in range(PARTS):
        rest.insert(len(rest) - PARTS + 1 + u, functools.partial(rows.cross, u))
    for u in range(PARTS):
        rest += [functools.partial(rows.round, u), functools.partial(halves.begin, u)]
    rest += halves.stages()[1:-1]
    first.pop(0)()
    matrix[col_here()] = total[...]
    products[0]()
    products[1]()
    first.pop(0)()
    products[2]()
    products[3]()
    rows.begin()
    for early, stage in zip(EARLY, first, strict=True):
        stage()
        for _ in range(early):
            rest.pop(0)()
    count = solved_ref.shape[0] // NB
    load_system(count, matrix.reshape(count * NB, count * NB), target_ref, aug)
    breaks = BREAKS * count
    beside = [[] for _ in range(breaks)]
    for i, stage in enumerate(rest):
        beside[i * breaks // len(rest)].append(stage)
    solve_system(count, solved_ref, aug, upper, sol, beside)
    halves.finish()
    rows.finish()
    band.finish()


def update_factors(band, scaled, basis, targets):
    n, ny, nz = lax.axis_size(ROW), lax.axis_size("y"), lax.axis_size("z")
    count, width = targets.shape
    height = count // n
    bands, blocks = band.shape[1] // NB, count // NB
    return pl.pallas_call(
        main_kernel,
        out_shape=[
            jax.ShapeDtypeStruct(targets.shape, jnp.bfloat16),
            jax.ShapeDtypeStruct((n, height, basis.shape[0]), jnp.bfloat16),
        ],
        in_specs=[pl.BlockSpec(memory_space=pltpu.VMEM)] * 4,
        out_specs=[pl.BlockSpec(memory_space=pltpu.VMEM)] * 2,
        scratch_shapes=[
            pltpu.VMEM((n, band.shape[0], NB), jnp.float32),
            pltpu.VMEM(band.shape, jnp.float32),
            pltpu.VMEM((n, height, basis.shape[0]), jnp.float32),
            pltpu.VMEM((lax.axis_size(COL), *band.shape), jnp.float32),
            pltpu.VMEM((2, ny - 1, height, basis.shape[0]), jnp.float32),
            pltpu.VMEM((height, basis.shape[0]), jnp.float32),
            pltpu.VMEM((blocks, NB, count + width), jnp.float32),
            pltpu.VMEM((blocks, NB, count + width), jnp.float32),
            pltpu.VMEM(targets.shape, jnp.float32),
            pltpu.SemaphoreType.DMA((bands,)), pltpu.SemaphoreType.DMA((n,)),
            pltpu.SemaphoreType.DMA((n - 1,)), pltpu.SemaphoreType.DMA((bands,)),
            *dma_pair(2 * PARTS * (ny - 1)), *dma_pair(PARTS),
            *dma_pair(Gather.count(nz, True, 1, PARTS)), *dma_pair(Gather.count(ny, False, 1, PARTS)),
        ],
        compiler_params=pltpu.CompilerParams(collective_id=1, has_side_effects=True, vmem_limit_bytes=56 << 20),
    )(band, scaled, basis, targets)


def picked(positions, size):
    return (positions[:, None] == jnp.arange(size, dtype=jnp.int32)[None, :]).astype(jnp.bfloat16)


def exact_rows(choice, array, dims):
    return lax.dot_general(choice, array, (dims, ((), ())), preferred_element_type=jnp.float32)


def payload_of(eigenbasis, weight, local_picks):
    slots, width = local_picks.shape[0], eigenbasis.shape[1]
    basis_rows = jnp.take(eigenbasis, local_picks, axis=0)
    columns = exact_rows(picked(local_picks, weight.shape[1]), weight, ((1,), (1,))).astype(jnp.bfloat16)
    columns = columns.reshape(ROWS16 - slots, -1)
    columns = jnp.pad(columns, ((0, 0), (0, width - columns.shape[1])))
    return jnp.concatenate([basis_rows, columns], axis=0)


def shards(weight, eigenbasis, eigenvalues, removed_local, counts):
    removed_count = KDEV * lax.axis_size(COL)
    slot_count = removed_local.shape[1]
    local_picks = removed_local[0]
    owners, ranks = compact_index(counts, removed_count)
    gathered = gather_col(payload_of(eigenbasis, weight, local_picks))
    shard_count, _, slab = gathered.shape
    compact = picked(owners * ROWS16 + ranks, shard_count * ROWS16)
    basis = exact_rows(compact, gathered.reshape(-1, slab), ((1,), (0,)))
    scaled = (basis / eigenvalues[None, :]).astype(jnp.bfloat16)
    basis = basis.astype(jnp.bfloat16)
    columns = gathered[:, slot_count:, : slot_count // (ROWS16 - slot_count) * weight.shape[0]]
    targets = exact_rows(
        picked(owners * slot_count + ranks, shard_count * slot_count), columns.reshape(-1, weight.shape[0]), ((1,), (0,))
    ).astype(jnp.bfloat16)
    first = lax.axis_index(COL) * KDEV
    band = exact_rows(lax.dynamic_slice_in_dim(scaled, first, KDEV), basis, ((1,), (1,)))
    band += exact_rows(lax.dynamic_slice_in_dim(basis, first, KDEV), scaled, ((1,), (1,)))
    solved_half, rows = update_factors(0.5 * band, scaled, eigenbasis, targets)
    change = exact_rows(solved_half, rows.reshape(removed_count, -1), ((0,), (0,)))
    return (weight.astype(jnp.float32) - change).astype(jnp.bfloat16)


def solution(mesh):
    torus = Mesh(mesh.devices.reshape(2, 8, 2, 8, 2), ("x_lo", "y", "x_hi", "z", "core"))
    return jax.shard_map(
        shards,
        mesh=torus,
        in_specs=(P(ROW, COL), P(COL, ROW), P(ROW), P(COL, None), P()),
        out_specs=P(ROW, COL),
        check_vma=False,
    )
```

```python
import functools
import jax
import jax.numpy as jnp
from jax import lax
from jax.experimental import pallas as pl
from jax.experimental.pallas import tpu as pltpu
from jax.sharding import Mesh
from jax.sharding import PartitionSpec as P

KDEV = 24
COL = ("x_hi", "z", "core")
ROW = ("x_lo", "y")
MESH = pl.DeviceIdType.MESH
ROWS16 = 48


def compact_index(counts, removed_count):
    shard_ids = jnp.arange(counts.shape[0], dtype=jnp.int32)
    shard_starts = jnp.sum(jnp.where(shard_ids[None, :] < shard_ids[:, None], counts[None, :], 0), axis=1)
    shard_ends = shard_starts + counts
    positions = jnp.arange(removed_count, dtype=jnp.int32)
    owners = jnp.sum((shard_ends[None, :] <= positions[:, None]).astype(jnp.int32), axis=1)
    owner_start = jnp.sum(
        jnp.where(owners[:, None] == shard_ids[None, :], shard_starts[None, :], 0), axis=1
    )
    return owners, positions - owner_start


HI = lax.Precision.HIGHEST
NB = 128
PAUSES = (2, 5, 8, 11)
BREAKS = len(PAUSES) + 2
PARTS = 3
EARLY = (0, 0, 1, 2, 2, 2, 2, 2, 0)

def lane_spread(tile, lane):
    return jnp.broadcast_to(tile[:, lane : lane + 1], tile.shape)


def invert_block(block, pause):
    lane = lax.broadcasted_iota(jnp.int32, (8, NB), 1)
    sub = lax.broadcasted_iota(jnp.int32, (8, NB), 0)
    count = NB // 8
    tiles = [block[8 * i : 8 * i + 8, :] for i in range(count)]
    for b in range(count):
        here = (lane >= 8 * b) & (lane < 8 * b + 8)
        pivots = [lane_spread(tiles[b], 8 * b + j) for j in range(8)]
        panel = jnp.where(here, jnp.where(lane - 8 * b == sub, 1.0, 0.0), tiles[b])
        for p in range(8):
            own = sub == p
            factor = pivots[p]
            inv = 1.0 / jnp.broadcast_to(factor[p : p + 1, :], (8, NB))

            def step(x):
                scaled = jnp.broadcast_to(x[p : p + 1, :], (8, NB)) * inv
                return jnp.where(own, scaled, x - factor * scaled)

            for q in range(p + 1, 8):
                pivots[q] = step(pivots[q])
            panel = step(panel)
        if b < count - 1:
            parts = [
                lane_spread(tiles[b + 1], 8 * b + j) * jnp.broadcast_to(panel[j : j + 1, :], (8, NB)) for j in range(8)
            ]
            while len(parts) > 1:
                parts = [parts[2 * m] + parts[2 * m + 1] for m in range(len(parts) // 2)]
            following = jnp.where(here, 0.0, tiles[b + 1]) - parts[0]
        spread = [panel]
        if b:
            spread.insert(0, jnp.zeros((8 * b, NB), jnp.float32))
        if b < count - 1:
            spread.append(jnp.zeros((NB - 8 * b - 8, NB), jnp.float32))
        change = jnp.dot(
            jnp.concatenate(tiles, axis=0), jnp.concatenate(spread, axis=0),
            preferred_element_type=jnp.float32, precision=HI,
        )
        for i in range(count):
            if i == b:
                tiles[i] = panel
            elif i == b + 1:
                tiles[i] = following
            else:
                tiles[i] = jnp.where(here, 0.0, tiles[i]) - change[8 * i : 8 * i + 8, :]
        if b in PAUSES:
            pause(PAUSES.index(b))
    return jnp.concatenate(tiles, axis=0)


def load_system(count, matrix, targets, aug):
    width = count * NB
    for i in range(count):
        aug[i, :, :width] = matrix[i * NB : (i + 1) * NB, :]
        aug[i, :, width:] = targets[i * NB : (i + 1) * NB, :].astype(jnp.float32)


def solve_system(count, out, aug, upper, sol, beside):
    width = count * NB

    def pause(k, which):
        for i in range(count):
            stages = beside[BREAKS * i + which]
            if stages:
                @pl.when(k == i)
                def _():
                    for stage in stages:
                        stage()

    def eliminate(k, _):
        here = pl.ds(pl.multiple_of(k * NB, NB), NB)
        inverse = invert_block(aug[k, :, here], functools.partial(pause, k))
        pause(k, BREAKS - 2)
        upper[k] = jnp.dot(inverse, aug[k], preferred_element_type=jnp.float32, precision=HI)

        def update(i, _):
            there = pl.ds(pl.multiple_of(i * NB, NB), NB)
            aug[i] -= lax.dot_general(
                aug[k, :, there], upper[k], (((0,), (0,)), ((), ())), preferred_element_type=jnp.float32, precision=HI
            )
            return 0

        lax.fori_loop(k + 1, count, update, 0)
        pause(k, BREAKS - 1)
        return 0

    lax.fori_loop(0, count, eliminate, 0)
    for k in range(count - 1, -1, -1):
        x = upper[k, :, width:]
        if k < count - 1:
            x = x - jnp.dot(
                upper[k, :, (k + 1) * NB : width], sol[(k + 1) * NB :, :],
                preferred_element_type=jnp.float32, precision=HI,
            )
        sol[k * NB : (k + 1) * NB, :] = x
        out[k * NB : (k + 1) * NB, :] = x.astype(jnp.bfloat16)


def remote(src, dst, sems, n, device):
    return pltpu.make_async_remote_copy(
        src_ref=src, dst_ref=dst, send_sem=sems[0].at[n], recv_sem=sems[1].at[n],
        device_id=device, device_id_type=MESH,
    )


def greet(devices):
    barrier = pltpu.get_barrier_semaphore()
    for device in devices:
        pl.semaphore_signal(barrier, inc=1, device_id=device, device_id_type=MESH)
    pl.semaphore_wait(barrier, len(devices))


class Gather:
    def __init__(self, source, out, sems, pair, ring, core, slot, near=0, cuts=None):
        self.source, self.out, self.sems = source, out, sems
        self.pair, self.ring, self.core, self.slot = pair, ring, core, slot
        self.near = near
        self.cuts = cuts or [pl.ds(0, source.shape[0])]
        self.p, self.r = lax.axis_index(pair), lax.axis_index(ring)
        self.k = lax.axis_index("core")
        self.n = lax.axis_size(ring)
        self.sends = self.plan()
        self.number = {what[0]: n for n, what in enumerate(self.sends)}

    def last(self, other, way):
        return self.n // 2 if (way == 1) != other else self.n // 2 - 1

    def plan(self):
        sends = []
        for u in range(len(self.cuts)):
            sends.append((("pair", u, 1, 0), False, 0, True))
            for way in (1, -1):
                for s in range(1, self.near + 1):
                    sends.append((("pair", u, way, s), False, -way * s, False))
                for s in range(1, self.last(False, way) + 1):
                    sends.append(((way, u, False, s), False, -way * (s - 1), s == 1))
                for s in range(self.near + 1, self.last(True, way) + 1):
                    sends.append(((way, u, True, s), True, -way * (s - 1), False))
            if self.core:
                for other in (False, True):
                    for offset in range(self.n):
                        sends.append((("core", u, other, offset), other, offset, not other and offset == 0))
        return sends

    @staticmethod
    def count(n, core, near=0, parts=1):
        return parts * (1 + 2 * near + (n - 1) + (n - 1 - 2 * near) + (2 * n if core else 0))

    def at(self, u, other, offset, sibling=False):
        p = 1 - self.p if other else self.p
        k = 1 - self.k if sibling else self.k
        return self.out.at[self.slot(p, lax.rem(self.r + offset + self.n, self.n), k), self.cuts[u]]

    def device(self, name):
        if name[0] == "pair":
            return {self.pair: 1 - self.p}
        if name[0] == "core":
            return {"core": 1 - self.k}
        return {self.ring: lax.rem(self.r + name[0] + self.n, self.n)}

    def copy(self, name):
        n = self.number[name]
        _, other, offset, own = self.sends[n]
        block = self.at(name[1], other, offset)
        return remote(self.source.at[self.cuts[name[1]]] if own else block, block, self.sems, n, self.device(name))

    def send(self, *name):
        self.copy(name).start()

    def arrived(self, dst, *name):
        remote(dst, dst, self.sems, self.number[name], self.device(name)).wait_recv()

    def share(self, u, other, offset):
        if self.core:
            self.send("core", u, other, offset % self.n)

    def begin(self, u):
        self.send("pair", u, 1, 0)
        for way in (1, -1):
            self.send(way, u, False, 1)
        self.share(u, False, 0)

    def cross(self, s, u):
        for way in (1, -1) if s else (1,):
            self.arrived(self.at(u, True, -way * s), "pair", u, way, s)
            for onward in (way,) if s else (1, -1):
                if s == self.near and s < self.last(True, onward):
                    self.send(onward, u, True, s + 1)
            self.share(u, True, -way * s)

    def advance(self, other, s, u):
        for way in (1, -1):
            if s > self.last(other, way):
                continue
            self.arrived(self.at(u, other, -way * s), way, u, other, s)
            if s < self.last(other, way):
                self.send(way, u, other, s + 1)
            if not other and s <= self.near:
                self.send("pair", u, way, s)
            self.share(u, other, -way * s)

    def finish(self):
        for u in range(len(self.cuts)):
            if self.core:
                for other in (False, True):
                    for offset in range(self.n):
                        self.arrived(self.at(u, other, offset, True), "core", u, other, offset)
        for what in self.sends:
            self.copy(what[0]).wait_send()

    def stages(self):
        own = [functools.partial(self.advance, False, s) for s in range(1, self.n // 2 + 1)]
        pair = [functools.partial(self.cross, s) for s in range(self.near + 1)]
        pair += [functools.partial(self.advance, True, s) for s in range(self.near + 1, self.n // 2 + 1)]
        mixed = [stage for both in zip(own, pair) for stage in both] + pair[len(own):]

        def each(stage):
            for u in range(len(self.cuts)):
                stage(u)

        return [functools.partial(each, stage) for stage in [self.begin, *mixed]] + [self.finish]


def col_slot(p, r, k):
    return (p * lax.axis_size("z") + r) * 2 + k


def row_slot(p, r, k):
    return p * lax.axis_size("y") + r


def col_neighbours():
    z, n = lax.axis_index("z"), lax.axis_size("z")
    return [
        {"core": 1 - lax.axis_index("core")},
        {"x_hi": 1 - lax.axis_index("x_hi")},
        {"z": lax.rem(z + 1, n)},
        {"z": lax.rem(z + n - 1, n)},
    ]


def col_here():
    return col_slot(lax.axis_index("x_hi"), lax.axis_index("z"), lax.axis_index("core"))


def row_cuts(ref, parts):
    rows = ref.shape[0] // parts
    return [pl.ds(u * rows, rows) for u in range(parts)]


def dma_pair(*shape):
    return [pltpu.SemaphoreType.DMA(shape), pltpu.SemaphoreType.DMA(shape)]


def gather_col_kernel(block_ref, out_ref, send, recv, local):
    mine = pltpu.make_async_copy(block_ref, out_ref.at[col_here()], local)
    mine.start()
    greet(col_neighbours())
    gather = Gather(block_ref, out_ref, (send, recv), "x_hi", "z", True, col_slot, 1, row_cuts(block_ref, PARTS))
    for stage in gather.stages():
        stage()
    mine.wait()


def gather_col(block):
    return pl.pallas_call(
        gather_col_kernel,
        out_shape=jax.ShapeDtypeStruct((lax.axis_size(COL), *block.shape), block.dtype),
        in_specs=[pl.BlockSpec(memory_space=pltpu.VMEM)],
        out_specs=pl.BlockSpec(memory_space=pltpu.VMEM),
        scratch_shapes=[*dma_pair(Gather.count(lax.axis_size("z"), True, 1, PARTS)), pltpu.SemaphoreType.DMA],
        compiler_params=pltpu.CompilerParams(collective_id=0, has_side_effects=True, vmem_limit_bytes=40 << 20),
    )(block)


class RowSum:
    def __init__(self, partial, ring_in, last_in, done, ring_sems, last_sems, parts):
        self.partial, self.ring_in, self.last_in, self.done = partial, ring_in, last_in, done
        self.ring_sems, self.last_sems = ring_sems, last_sems
        self.x, self.y, self.n = lax.axis_index("x_lo"), lax.axis_index("y"), lax.axis_size("y")
        rows = partial.shape[1] // parts
        self.cuts = [pl.ds(u * rows, rows) for u in range(parts)]

    def term(self, w, hops, u):
        way = 1 - 2 * w
        return self.partial.at[w * self.n + lax.rem(self.y - way * hops + 2 * self.n, self.n), self.cuts[u]]

    def copy(self, w, u, s):
        src = self.term(w, 1, u) if s == 0 else self.ring_in.at[w, s - 1, self.cuts[u]]
        n = (w * len(self.cuts) + u) * (self.n - 1) + s
        target = {"y": lax.rem(self.y + 1 - 2 * w + self.n, self.n)}
        return remote(src, self.ring_in.at[w, s, self.cuts[u]], self.ring_sems, n, target)

    def every(self):
        return [(w, u) for u in range(len(self.cuts)) for w in range(2)]

    def begin(self):
        for w, u in self.every():
            self.copy(w, u, 0).start()

    def advance(self, s, u):
        for w in range(2):
            self.copy(w, u, s).wait_recv()
            self.ring_in[w, s, self.cuts[u]] += self.term(w, 2 + s, u)[...]
            if s < self.n - 2:
                self.copy(w, u, s + 1).start()

    def last(self, u):
        src = self.ring_in.at[1 - self.x, self.n - 2, self.cuts[u]]
        return remote(src, self.last_in.at[self.cuts[u]], self.last_sems, u, {"x_lo": 1 - self.x})

    def cross(self, u):
        self.last(u).start()

    def round(self, u):
        self.last(u).wait_recv()
        value = self.ring_in[self.x, self.n - 2, self.cuts[u]] + self.last_in[self.cuts[u]]
        self.done[row_slot(self.x, self.y, 0), self.cuts[u]] = value.astype(jnp.bfloat16)

    def finish(self):
        for w, u in self.every():
            for s in range(self.n - 1):
                self.copy(w, u, s).wait_send()
        for u in range(len(self.cuts)):
            self.last(u).wait_send()

    def steps(self):
        return [functools.partial(self.advance, s, u) for s in range(self.n - 1) for u in range(len(self.cuts))]


class BandSum:
    def __init__(self, band, band_in, total, in_sems, out_sems):
        self.band, self.band_in, self.total = band, band_in, total
        self.in_sems, self.out_sems = in_sems, out_sems
        self.x, self.y, self.n = lax.axis_index("x_lo"), lax.axis_index("y"), lax.axis_size("y")
        self.bands = band.shape[1] // NB

    def peers(self):
        return [
            (lax.rem(self.x + dx, 2), lax.rem(self.y + dy, self.n))
            for dx in range(2) for dy in range(self.n) if dx or dy
        ]

    def home(self, p):
        return jnp.logical_and(self.x == p % 2, self.y == p)

    def inward(self, p, source):
        target = {"x_lo": jnp.int32(p % 2), "y": jnp.int32(p)}
        return pltpu.make_async_remote_copy(
            src_ref=self.band.at[:, pl.ds(p * NB, NB)], dst_ref=self.band_in.at[source],
            send_sem=self.in_sems[0].at[p], recv_sem=self.in_sems[1].at[source], device_id=target, device_id_type=MESH,
        )

    def outward(self, p, number, peer):
        cut = self.total.at[:, pl.ds(p * NB, NB)]
        return pltpu.make_async_remote_copy(
            src_ref=cut, dst_ref=cut, send_sem=self.out_sems[0].at[number], recv_sem=self.out_sems[1].at[p],
            device_id={"x_lo": peer[0], "y": peer[1]}, device_id_type=MESH,
        )

    def begin(self):
        here = row_slot(self.x, self.y, 0)
        for p in range(self.bands):
            @pl.when(jnp.logical_not(self.home(p)))
            def _():
                self.inward(p, here).start()

    def sum_home(self):
        for p in range(self.bands):
            @pl.when(self.home(p))
            def _():
                total = self.band[:, p * NB : (p + 1) * NB]
                for x, y in self.peers():
                    source = row_slot(x, y, 0)
                    self.inward(p, source).wait_recv()
                    total = total + self.band_in[source]
                self.total[:, p * NB : (p + 1) * NB] = total
                for number, peer in enumerate(self.peers()):
                    self.outward(p, number, peer).start()

    def arrive(self):
        for p in range(self.bands):
            @pl.when(jnp.logical_not(self.home(p)))
            def _():
                self.outward(p, 0, (jnp.int32(p % 2), jnp.int32(p))).wait_recv()

    def finish(self):
        here = row_slot(self.x, self.y, 0)
        for p in range(self.bands):
            @pl.when(jnp.logical_not(self.home(p)))
            def _():
                self.inward(p, here).wait_send()

            @pl.when(self.home(p))
            def _():
                for number, peer in enumerate(self.peers()):
                    self.outward(p, number, peer).wait_send()


def partial_rows(scaled, basis, partial, chunk):
    n, height, width = partial.shape
    calls = []
    for i in range(0, n, chunk):
        def call(i=i):
            value = lax.dot_general(
                scaled[i * height : (i + chunk) * height, :], basis[...], (((1,), (1,)), ((), ())),
                preferred_element_type=jnp.float32,
            )
            partial[i : i + chunk] = value.reshape(chunk, height, width)
        calls.append(call)
    return calls


def main_kernel(band_ref, scaled_ref, basis_ref, target_ref, solved_ref, rows_ref, band_in, total, partial, matrix,
                ring_in, last_in, aug, upper, sol, *sems):
    pairs = [(sems[2 * i], sems[2 * i + 1]) for i in range(len(sems) // 2)]
    band = BandSum(band_ref, band_in, total, pairs[0], pairs[1])
    rows = RowSum(partial, ring_in, last_in, rows_ref, pairs[2], pairs[3], PARTS)
    spread = Gather(total, matrix, pairs[4], "x_hi", "z", True, col_slot, 1, row_cuts(total, PARTS))
    own_rows = rows_ref.at[row_slot(rows.x, rows.y, 0)]
    halves = Gather(own_rows, rows_ref, pairs[5], "x_lo", "y", False, row_slot, 1, row_cuts(own_rows, PARTS))
    greet([{"x_lo": x, "y": y} for x, y in band.peers()] + col_neighbours())
    products = partial_rows(scaled_ref, basis_ref, partial, 4)
    band.begin()
    band.sum_home()
    band.arrive()
    first, rest = spread.stages(), rows.steps()
    for u in range(PARTS):
        rest.insert(len(rest) - PARTS + 1 + u, functools.partial(rows.cross, u))
    for u in range(PARTS):
        rest += [functools.partial(rows.round, u), functools.partial(halves.begin, u)]
    rest += halves.stages()[1:-1]
    first.pop(0)()
    matrix[col_here()] = total[...]
    products[0]()
    products[1]()
    first.pop(0)()
    products[2]()
    products[3]()
    rows.begin()
    for early, stage in zip(EARLY, first, strict=True):
        stage()
        for _ in range(early):
            rest.pop(0)()
    count = solved_ref.shape[0] // NB
    load_system(count, matrix.reshape(count * NB, count * NB), target_ref, aug)
    breaks = BREAKS * count
    beside = [[] for _ in range(breaks)]
    for i, stage in enumerate(rest):
        beside[i * breaks // len(rest)].append(stage)
    solve_system(count, solved_ref, aug, upper, sol, beside)
    halves.finish()
    rows.finish()
    band.finish()


def update_factors(band, scaled, basis, targets):
    n, ny, nz = lax.axis_size(ROW), lax.axis_size("y"), lax.axis_size("z")
    count, width = targets.shape
    height = count // n
    bands, blocks = band.shape[1] // NB, count // NB
    return pl.pallas_call(
        main_kernel,
        out_shape=[
            jax.ShapeDtypeStruct(targets.shape, jnp.bfloat16),
            jax.ShapeDtypeStruct((n, height, basis.shape[0]), jnp.bfloat16),
        ],
        in_specs=[pl.BlockSpec(memory_space=pltpu.VMEM)] * 4,
        out_specs=[pl.BlockSpec(memory_space=pltpu.VMEM)] * 2,
        scratch_shapes=[
            pltpu.VMEM((n, band.shape[0], NB), jnp.float32),
            pltpu.VMEM(band.shape, jnp.float32),
            pltpu.VMEM((n, height, basis.shape[0]), jnp.float32),
            pltpu.VMEM((lax.axis_size(COL), *band.shape), jnp.float32),
            pltpu.VMEM((2, ny - 1, height, basis.shape[0]), jnp.float32),
            pltpu.VMEM((height, basis.shape[0]), jnp.float32),
            pltpu.VMEM((blocks, NB, count + width), jnp.float32),
            pltpu.VMEM((blocks, NB, count + width), jnp.float32),
            pltpu.VMEM(targets.shape, jnp.float32),
            pltpu.SemaphoreType.DMA((bands,)), pltpu.SemaphoreType.DMA((n,)),
            pltpu.SemaphoreType.DMA((n - 1,)), pltpu.SemaphoreType.DMA((bands,)),
            *dma_pair(2 * PARTS * (ny - 1)), *dma_pair(PARTS),
            *dma_pair(Gather.count(nz, True, 1, PARTS)), *dma_pair(Gather.count(ny, False, 1, PARTS)),
        ],
        compiler_params=pltpu.CompilerParams(collective_id=1, has_side_effects=True, vmem_limit_bytes=56 << 20),
    )(band, scaled, basis, targets)


def picked(positions, size):
    return (positions[:, None] == jnp.arange(size, dtype=jnp.int32)[None, :]).astype(jnp.bfloat16)


def exact_rows(choice, array, dims):
    return lax.dot_general(choice, array, (dims, ((), ())), preferred_element_type=jnp.float32)


def payload_of(eigenbasis, weight, local_picks):
    slots, width = local_picks.shape[0], eigenbasis.shape[1]
    basis_rows = jnp.take(eigenbasis, local_picks, axis=0)
    columns = exact_rows(picked(local_picks, weight.shape[1]), weight, ((1,), (1,))).astype(jnp.bfloat16)
    columns = columns.reshape(ROWS16 - slots, -1)
    columns = jnp.pad(columns, ((0, 0), (0, width - columns.shape[1])))
    return jnp.concatenate([basis_rows, columns], axis=0)


def shards(weight, eigenbasis, eigenvalues, removed_local, counts):
    removed_count = KDEV * lax.axis_size(COL)
    slot_count = removed_local.shape[1]
    local_picks = removed_local[0]
    owners, ranks = compact_index(counts, removed_count)
    gathered = gather_col(payload_of(eigenbasis, weight, local_picks))
    shard_count, _, slab = gathered.shape
    compact = picked(owners * ROWS16 + ranks, shard_count * ROWS16)
    basis = exact_rows(compact, gathered.reshape(-1, slab), ((1,), (0,)))
    scaled = (basis / eigenvalues[None, :]).astype(jnp.bfloat16)
    basis = basis.astype(jnp.bfloat16)
    columns = gathered[:, slot_count:, : slot_count // (ROWS16 - slot_count) * weight.shape[0]]
    targets = exact_rows(
        picked(owners * slot_count + ranks, shard_count * slot_count), columns.reshape(-1, weight.shape[0]), ((1,), (0,))
    ).astype(jnp.bfloat16)
    first = lax.axis_index(COL) * KDEV
    band = exact_rows(lax.dynamic_slice_in_dim(scaled, first, KDEV), basis, ((1,), (1,)))
    band += exact_rows(lax.dynamic_slice_in_dim(basis, first, KDEV), scaled, ((1,), (1,)))
    solved_half, rows = update_factors(0.5 * band, scaled, eigenbasis, targets)
    change = exact_rows(solved_half, rows.reshape(removed_count, -1), ((0,), (0,)))
    return (weight.astype(jnp.float32) - change).astype(jnp.bfloat16)


def solution(mesh):
    torus = Mesh(mesh.devices.reshape(2, 8, 2, 8, 2), ("x_lo", "y", "x_hi", "z", "core"))
    return jax.shard_map(
        shards,
        mesh=torus,
        in_specs=(P(ROW, COL), P(COL, ROW), P(ROW), P(COL, None), P()),
        out_specs=P(ROW, COL),
        check_vma=False,
    )
```
